32 devices in a mesh: dp: 4 (over z), expert: 8 (over y, x, core).
Axes of the slice: x: 2, y: 2, z: 4, core: 2. Of those that a mesh axis runs over, the one named last changes fastest.
Arguments:
- ids: int32 [8192], P('dp'), may hold values from 0 to 31999
- targets: int32 [8192], P('dp'), may hold values from 0 to 31999
- loss_mask: int32 [8192], replicated, may hold values from 0 to 1
- domain_ids: int32 [4], replicated, may hold values from 0 to 3
- expert_lists: int32 [4, 8, 8, 128], P('dp', 'expert'), may hold values from -1 to 255, as said below
- tables: float32 [2, 32000, 768], P(None, ('expert', 'dp'))
- tables_m: float32 [2, 32000, 768], P(None, ('expert', 'dp'))
- tables_v: float32 [2, 32000, 768], P(None, ('expert', 'dp'))
- attn: float32 [4, 768, 768], P(None, 'dp')
- attn_m: float32 [4, 768, 768], P(None, 'dp')
- attn_v: float32 [4, 768, 768], P(None, 'dp')
- experts: float32 [8, 2, 768, 3072], P('expert', None, None, 'dp')
- experts_m: float32 [8, 2, 768, 3072], P('expert', None, None, 'dp')
- experts_v: float32 [8, 2, 768, 3072], P('expert', None, None, 'dp')
- router: float32 [768, 8], replicated, may hold values from -0.109375 to 0.109375
- router_m: float32 [768, 8], replicated
- router_v: float32 [768, 8], replicated
- gains: float32 [3, 768], replicated
- gains_m: float32 [3, 768], replicated
- gains_v: float32 [3, 768], replicated
Outputs:
- domain_sums: float32 [4], replicated
- domain_counts: float32 [4], replicated
- grad_norm: float32 [], replicated
- tables_first: float32 [2, 32000, 768], P(None, ('expert', 'dp'))
- tables_second: float32 [2, 32000, 768], P(None, ('expert', 'dp'))
- tables_new: float32 [2, 32000, 768], P(None, ('expert', 'dp'))
- tables_copy: bfloat16 [2, 32000, 768], P(None, ('expert', 'dp'))
- attn_first: float32 [4, 768, 768], P(None, 'dp')
- attn_second: float32 [4, 768, 768], P(None, 'dp')
- attn_new: float32 [4, 768, 768], P(None, 'dp')
- attn_copy: bfloat16 [4, 768, 768], P(None, 'dp')
- experts_first: float32 [8, 2, 768, 3072], P('expert', None, None, 'dp')
- experts_second: float32 [8, 2, 768, 3072], P('expert', None, None, 'dp')
- experts_new: float32 [8, 2, 768, 3072], P('expert', None, None, 'dp')
- experts_copy: bfloat16 [8, 2, 768, 3072], P('expert', None, None, 'dp')
- router_first: float32 [768, 8], replicated
- router_second: float32 [768, 8], replicated
- router_new: float32 [768, 8], replicated
- router_copy: bfloat16 [768, 8], replicated
- gains_first: float32 [3, 768], replicated
- gains_second: float32 [3, 768], replicated
- gains_new: float32 [3, 768], replicated
- gains_copy: bfloat16 [3, 768], replicated
The draws below stay inside these ranges and needn't reach their ends.
Inputs may be any that keep to these rules, and one draw needn't show every extreme that they name: `expert_lists`: in every list of one batch group, source device and expert the filled slots come first and name distinct local token rows; in each batch group one expert has every slot filled from every source device.
All inputs are finite; a program needn't handle non-finite values.
Results may differ from the reference program's by a relative error of at most 0.033.
Values may be sent and summed in bfloat16 or wider, within the bound.
No kernel may reach another device: no remote copies, remote signals or barrier semaphores. Data moves between devices by JAX's collectives and lax.ppermute only.
A program may use at most 320 MiB of HBM per device.

```python
import math
from functools import partial
import jax
import jax.numpy as jnp
from jax import lax

D = 768
HEADS = 12
HEAD_DIM = 64
FF = 3072
VOCAB = 32000
TOK_DEV = 256
SEQ = 2048
NDOM = 4
STEP = 10
EXPERTS = 8
SLOT = 128
GROUP_TOK = 2048
TOKENS = 8192
SEQS = 4


def moment(key, shape, scale, second):
    if second:
        return scale * scale * jnp.exp(jax.random.uniform(key, shape, jnp.float32, 0.0, math.log(4.0)))
    return scale * jax.random.normal(key, shape, jnp.float32)


def table_scale():
    return 0.5 * (2.0 * VOCAB * D) ** (-0.5)


def attn_scale():
    return 0.4 * (4.0 * D * D) ** (-0.5)


def expert_scale():
    return 0.5 * (2.0 * EXPERTS * D * FF) ** (-0.5)


def router_scale():
    return 0.2 * (1.0 * D * EXPERTS) ** (-0.5)


def gain_scale():
    return 0.1 * (3.0 * D) ** (-0.5)


def draw_loss_mask(key, part):
    key = jax.random.fold_in(key, 5)
    place = jnp.arange(TOKENS)
    inner = place % GROUP_TOK
    outer = place // GROUP_TOK
    limit = 150 + 300 * inner // GROUP_TOK + 300 * outer // (TOKENS // GROUP_TOK)
    return (jax.random.randint(key, (TOKENS,), 0, 1000) < limit).astype(jnp.int32)


def draw_expert_lists(key, part):
    key = jax.random.fold_in(key, 7)
    key_one, key_two, key_three, key_four = jax.random.split(key, 4)
    groups = TOKENS // GROUP_TOK
    sources = GROUP_TOK // TOK_DEV
    popular = jnp.left_shift(1, jax.random.randint(key_one, (groups, sources, TOK_DEV), 0, 6))
    noise = jax.random.randint(key_two, (groups, sources, EXPERTS, TOK_DEV), 1, 1024)
    score = noise * popular[:, :, None, :] * TOK_DEV + jnp.arange(TOK_DEV)[None, None, None, :]
    _, picked = lax.top_k(score, SLOT)
    count = jax.random.randint(key_three, (groups, sources, EXPERTS), SLOT // 4, SLOT + 1)
    full = jax.random.randint(key_four, (groups,), 0, EXPERTS)
    count = jnp.where(jnp.arange(EXPERTS)[None, None, :] == full[:, None, None], SLOT, count)
    return jnp.where(jnp.arange(SLOT)[None, None, None, :] < count[..., None], picked, -1).astype(jnp.int32)


def draw_tables(key, part):
    key = jax.random.fold_in(key, 11)
    key_one, key_two = jax.random.split(key)
    base = jax.random.normal(key_one, (2, VOCAB, D), jnp.float32)
    top_spread = 3.0
    rise = 1.0 + (top_spread - 1.0) * jnp.arange(VOCAB, dtype=jnp.float32) / VOCAB
    jitter = jax.random.uniform(key_two, (VOCAB,), jnp.float32, 0.9, 1.1)
    embed_part = base[0] * 0.1
    head_part = base[1] * (rise * jitter)[:, None] / (1.2 * math.sqrt(D))
    return jnp.stack([embed_part, head_part])


def draw_tables_m(key, part):
    key = jax.random.fold_in(key, 12)
    return moment(key, (2, VOCAB, D), table_scale(), False)


def draw_tables_v(key, part):
    key = jax.random.fold_in(key, 13)
    return moment(key, (2, VOCAB, D), table_scale(), True)


def draw_attn(key, part):
    key = jax.random.fold_in(key, 21)
    base = jax.random.normal(key, (4, D, D), jnp.float32)
    factors = jnp.array([1.1, 1.1, 1.0, 6.0], jnp.float32) / math.sqrt(D)
    return base * factors[:, None, None]


def draw_attn_m(key, part):
    key = jax.random.fold_in(key, 22)
    return moment(key, (4, D, D), attn_scale(), False)


def draw_attn_v(key, part):
    key = jax.random.fold_in(key, 23)
    return moment(key, (4, D, D), attn_scale(), True)


def draw_experts(key, part):
    key = jax.random.fold_in(key, 31)
    base = jax.random.normal(key, (EXPERTS, 2, D, FF), jnp.float32)
    factors = jnp.array([1.0 / math.sqrt(D), 10.0 / math.sqrt(FF)], jnp.float32)
    return base * factors[None, :, None, None]


def draw_experts_m(key, part):
    key = jax.random.fold_in(key, 32)
    return moment(key, (EXPERTS, 2, D, FF), expert_scale(), False)


def draw_experts_v(key, part):
    key = jax.random.fold_in(key, 33)
    return moment(key, (EXPERTS, 2, D, FF), expert_scale(), True)


def draw_router_m(key, part):
    key = jax.random.fold_in(key, 42)
    return moment(key, (D, EXPERTS), router_scale(), False)


def draw_router_v(key, part):
    key = jax.random.fold_in(key, 43)
    return moment(key, (D, EXPERTS), router_scale(), True)


def draw_gains(key, part):
    key = jax.random.fold_in(key, 51)
    start, reach = (0.6, 1.2)
    rise = start + reach * jnp.arange(D, dtype=jnp.float32) / D
    jitter = jax.random.uniform(key, (3, D), jnp.float32, 0.85, 1.15)
    return rise[None, :] * jitter


def draw_gains_m(key, part):
    key = jax.random.fold_in(key, 52)
    return moment(key, (3, D), gain_scale(), False)


def draw_gains_v(key, part):
    key = jax.random.fold_in(key, 53)
    return moment(key, (3, D), gain_scale(), True)


def touch_ends(values, rng, least, largest):
    longest = values.shape.index(max(values.shape))
    spots = []
    for shift in (0, 1):
        where = [jax.random.randint(jax.random.fold_in(rng, axis), (), 0, length) for axis, length in enumerate(values.shape)]
        where[longest] = (where[longest] + shift) % values.shape[longest]
        spots.append(tuple(where))
    return values.at[spots[0]].set(least).at[spots[1]].set(largest)


def scatter_about(own_key, shape, deviation, most, held_as=jnp.bfloat16):
    return jnp.clip(deviation * jax.random.normal(own_key, shape, jnp.float32), -most, most).astype(held_as)


def setup_inputs(seed: int = 0) -> dict:
    streams_of = jax.random.split(jax.random.key(seed), 21)
    ids = touch_ends(jax.random.randint(streams_of[0], (TOKENS,), 0, VOCAB), jax.random.fold_in(streams_of[0], 1), 0, VOCAB - 1).astype(jnp.int32)
    targets = touch_ends(jax.random.randint(streams_of[1], (TOKENS,), 0, VOCAB), jax.random.fold_in(streams_of[1], 1), 0, VOCAB - 1).astype(jnp.int32)
    loss_mask = draw_loss_mask(jax.random.fold_in(streams_of[20], 71), 0)
    domain_ids = touch_ends(jax.random.randint(streams_of[3], (SEQS,), 0, NDOM), jax.random.fold_in(streams_of[3], 1), 0, NDOM - 1).astype(jnp.int32)
    expert_lists = draw_expert_lists(jax.random.fold_in(streams_of[20], 71), 0)
    tables = draw_tables(jax.random.fold_in(streams_of[20], 71), 0)
    tables_m = draw_tables_m(jax.random.fold_in(streams_of[20], 71), 0)
    tables_v = draw_tables_v(jax.random.fold_in(streams_of[20], 71), 0)
    attn = draw_attn(jax.random.fold_in(streams_of[20], 71), 0)
    attn_m = draw_attn_m(jax.random.fold_in(streams_of[20], 71), 0)
    attn_v = draw_attn_v(jax.random.fold_in(streams_of[20], 71), 0)
    experts = draw_experts(jax.random.fold_in(streams_of[20], 71), 0)
    experts_m = draw_experts_m(jax.random.fold_in(streams_of[20], 71), 0)
    experts_v = draw_experts_v(jax.random.fold_in(streams_of[20], 71), 0)
    router = scatter_about(streams_of[14], (D, EXPERTS), (4 * D) ** -0.5, 0.109375, jnp.float32)
    router_m = draw_router_m(jax.random.fold_in(streams_of[20], 71), 0)
    router_v = draw_router_v(jax.random.fold_in(streams_of[20], 71), 0)
    gains = draw_gains(jax.random.fold_in(streams_of[20], 71), 0)
    gains_m = draw_gains_m(jax.random.fold_in(streams_of[20], 71), 0)
    gains_v = draw_gains_v(jax.random.fold_in(streams_of[20], 71), 0)
    return dict(ids=ids, targets=targets, loss_mask=loss_mask, domain_ids=domain_ids, expert_lists=expert_lists, tables=tables, tables_m=tables_m, tables_v=tables_v, attn=attn, attn_m=attn_m, attn_v=attn_v, experts=experts, experts_m=experts_m, experts_v=experts_v, router=router, router_m=router_m, router_v=router_v, gains=gains, gains_m=gains_m, gains_v=gains_v)


@jax.custom_vjp
def low(v):
    return lax.optimization_barrier(v.astype(jnp.bfloat16)).astype(jnp.float32)

@jax.custom_vjp
def low_back(v):
    return v

def low_keep(v):
    return (low(v), None)

def low_pass(kept, grad):
    return (grad,)

def back_keep(v):
    return (v, None)

def back_low(kept, grad):
    return (low(grad),)
low.defvjp(low_keep, low_pass)
low_back.defvjp(back_keep, back_low)
NORM_EPS = 1e-05
BETA = 0.5
ADAM_EPS = 1e-08
CLIP = 1.0
HIGHEST = lax.Precision.HIGHEST

def normed(values, gain):
    return values * lax.rsqrt(lax.optimization_barrier(jnp.mean(values * values, axis=-1, keepdims=True)) + NORM_EPS) * gain

def attend_seq(inputs):
    queries, keys, values = inputs
    scale = queries.shape[-1] ** (-0.5)
    scores = low_back(jnp.einsum('qhd,khd->hqk', queries, keys, precision=HIGHEST) * scale)
    place = jnp.arange(queries.shape[0])
    scores = jnp.where((place[None, :] <= place[:, None])[None], scores, -1e+30)
    weights = low(jax.nn.softmax(scores, axis=-1))
    return jnp.einsum('hqk,khd->qhd', weights, values, precision=HIGHEST)

def expert_run(inputs):
    rows, w_up, w_down = inputs
    pre = low_back(jnp.dot(rows, w_up, precision=HIGHEST))
    hidden = low(jax.nn.gelu(pre, approximate=True))
    produced = jnp.dot(hidden, w_down.T, precision=HIGHEST)
    return low(low_back(produced))

def head_loss(head, inputs):
    rows, target_rows = inputs
    logits = low_back(jnp.dot(rows, head.T, precision=HIGHEST))
    top = lax.optimization_barrier(jnp.max(logits, axis=-1))
    logsum = top + jnp.log(lax.optimization_barrier(jnp.sum(jnp.exp(logits - top[:, None]), axis=-1)))
    picked = jnp.take_along_axis(logits, target_rows[:, None], axis=1)[:, 0]
    return logsum - picked

def adam(weight, grad, first, second, rate, decay):
    first = BETA * first + (1.0 - BETA) * grad
    second = BETA * second + (1.0 - BETA) * grad * grad
    correct = 1.0 - BETA ** STEP
    weight = weight - rate * (first / correct / (jnp.sqrt(second / correct) + ADAM_EPS) + decay * weight)
    return (first, second, weight, weight.astype(jnp.bfloat16))

def reference(ids, targets, loss_mask, domain_ids, expert_lists, tables, tables_m, tables_v, attn, attn_m, attn_v, experts, experts_m, experts_v, router, router_m, router_v, gains, gains_m, gains_v):
    place = jnp.arange(TOKENS)
    domain_of = domain_ids[place // SEQ]
    hits = ((domain_of[:, None] == jnp.arange(NDOM)[None, :]) & (loss_mask[:, None] > 0)).astype(jnp.float32)
    counts = lax.optimization_barrier(jnp.sum(hits, axis=0))
    domain_weight = 10.0 * (NDOM - jnp.arange(NDOM)).astype(jnp.float32) / jnp.maximum(counts, 1.0)
    token_weight = lax.optimization_barrier(jnp.sum(hits * domain_weight[None, :], axis=1))
    groups = expert_lists.shape[0]
    sources = expert_lists.shape[1]
    filled = expert_lists >= 0
    offsets = jnp.arange(groups)[:, None] * GROUP_TOK + jnp.arange(sources)[None, :] * TOK_DEV
    token_index = jnp.where(filled, expert_lists + offsets[:, :, None, None], 0)
    token_index = jnp.transpose(token_index, (2, 0, 1, 3)).reshape(EXPERTS, -1)
    slot_valid = jnp.transpose(filled, (2, 0, 1, 3)).reshape(EXPERTS, -1).astype(jnp.float32)
    head_block = min(512, TOKENS)

    def forward(tables, attn, experts, router, gains):
        tables_b = low(tables)
        attn_b = low(attn)
        experts_b = low(experts)
        router_b = low(router)
        embedded = low_back(jnp.take(tables_b[0], ids, axis=0))
        normed_a = low(normed(embedded, gains[0]))
        projected = jnp.einsum('td,kde->kte', normed_a, attn_b[:3], precision=HIGHEST)
        projected = low(low_back(projected)).reshape(3, SEQS, SEQ, HEADS, HEAD_DIM)
        mixed = lax.map(jax.checkpoint(attend_seq), (projected[0], projected[1], projected[2]))
        mixed = low(low_back(mixed.reshape(TOKENS, D)))
        branch = low_back(jnp.dot(mixed, attn_b[3], precision=HIGHEST))
        resid_one = embedded + branch
        normed_b = low(normed(resid_one, gains[1]))
        gates = jax.nn.softmax(low_back(jnp.dot(normed_b, router_b, precision=HIGHEST)), axis=-1)
        rows = low_back(jnp.take(normed_b, token_index, axis=0) * slot_valid[..., None])
        produced = lax.map(jax.checkpoint(expert_run), (rows, experts_b[:, 0], experts_b[:, 1]))
        slot_gates = gates[token_index, jnp.arange(EXPERTS)[:, None]] * slot_valid
        mixture = jnp.zeros((TOKENS, D), jnp.float32).at[token_index.reshape(-1)].add((slot_gates[..., None] * produced).reshape(-1, D))
        resid_two = resid_one + mixture
        normed_c = low(normed(resid_two, gains[2]))
        losses = lax.map(jax.checkpoint(partial(head_loss, tables_b[1])), (normed_c.reshape(-1, head_block, D), targets.reshape(-1, head_block)))
        losses = losses.reshape(-1)
        return (jnp.sum(token_weight * losses), lax.optimization_barrier(jnp.sum(hits * losses[:, None], axis=0)))
    loss, pull, domain_sums = jax.vjp(forward, tables, attn, experts, router, gains, has_aux=True)
    grads = pull(jnp.ones((), jnp.float32))
    squares = sum((jnp.sum(grad * grad) for grad in grads))
    grad_norm = jnp.sqrt(squares)
    factor = jnp.minimum(1.0, CLIP / (grad_norm + 1e-06))
    grad_tables, grad_attn, grad_experts, grad_router, grad_gains = [grad * factor for grad in grads]
    tables_out = adam(tables, grad_tables, tables_m, tables_v, 0.1, 0.01)
    attn_out = adam(attn, grad_attn, attn_m, attn_v, 0.1, 0.01)
    experts_out = adam(experts, grad_experts, experts_m, experts_v, 0.1, 0.01)
    router_out = adam(router, grad_router, router_m, router_v, 0.04, 0.01)
    gains_out = adam(gains, grad_gains, gains_m, gains_v, 0.4, 0.0)
    return (domain_sums, counts, grad_norm, tables_out[0], tables_out[1], tables_out[2], tables_out[3], attn_out[0], attn_out[1], attn_out[2], attn_out[3], experts_out[0], experts_out[1], experts_out[2], experts_out[3], router_out[0], router_out[1], router_out[2], router_out[3], gains_out[0], gains_out[1], gains_out[2], gains_out[3])
```

```python
import functools

import jax
import jax.numpy as jnp
from jax import lax
from jax.experimental import pallas as pl
from jax.experimental.pallas import tpu as pltpu
from jax.sharding import PartitionSpec as P

HEADS = 12
SEQ = 2048
NDOM = 4
STEP = 10


NORM_EPS = 1e-05
BETA = 0.5
ADAM_EPS = 1e-08
CLIP = 1.0
MASKED = -1e30
BF = jnp.bfloat16
F32 = jnp.float32
VMEM_BYTES = 56 * 1024 * 1024


def normed(values, gain):
    return values * lax.rsqrt(jnp.mean(values * values, axis=-1, keepdims=True) + NORM_EPS) * gain


def norm_back(values, gain, grad):
    _, pull = jax.vjp(normed, values, gain)
    return pull(grad)


def gelu(values):
    return jax.nn.gelu(values, approximate=True)


def adam(weight, grad, first, second, rate, decay):
    first = BETA * first + (1.0 - BETA) * grad
    second = BETA * second + (1.0 - BETA) * grad * grad
    correct = 1.0 - BETA**STEP
    weight = weight - rate * (
        first / correct / (jnp.sqrt(second / correct) + ADAM_EPS) + decay * weight
    )
    return (first, second, weight, weight.astype(BF))


def dot(a, b, contract):
    return lax.dot_general(a, b, ((contract[0], contract[1]), ((), ())), preferred_element_type=F32)


def dot_nn(a, b):
    return dot(a, b, ((1,), (0,)))


def dot_nt(a, b):
    return dot(a, b, ((1,), (1,)))


def dot_tn(a, b):
    return dot(a, b, ((0,), (0,)))


def swap(array, bits, axis):
    pairs = [(i, i ^ bits) for i in range(lax.axis_size(axis))]
    return lax.ppermute(array, axis, pairs)


def turn(array, steps):
    count = lax.axis_size("dp")
    return lax.ppermute(array, "dp", [(i, (i + steps) % count) for i in range(count)])


def quick_expert():
    return lax.axis_size("expert") == 8


def quick_dp():
    return lax.axis_size("dp") == 4


def block_order():
    count = lax.axis_size("expert")
    if quick_expert():
        return lax.axis_index("expert") ^ jnp.arange(count)
    return jnp.arange(count)


def gather_blocks(rows):
    if not quick_expert():
        gathered = lax.all_gather(rows, "expert")
        return [gathered[i] for i in range(lax.axis_size("expert"))]
    half = rows.shape[0] // 2
    one, two, four = (swap(rows, bits, "expert") for bits in (1, 2, 4))
    six_a = swap(two[:half], 4, "expert")
    six_b = swap(four[half:], 2, "expert")
    three = swap(two, 1, "expert")
    five = swap(four, 1, "expert")
    seven_a = swap(six_a, 1, "expert")
    seven_b = swap(six_b, 1, "expert")
    return [
        rows,
        one,
        two,
        three,
        four,
        five,
        jnp.concatenate([six_a, six_b]),
        jnp.concatenate([seven_a, seven_b]),
    ]


def gather_rows(rows):
    return jnp.concatenate(gather_blocks(rows))


def sum_blocks(blocks):
    if not quick_expert():
        return lax.psum_scatter(
            jnp.stack(blocks), "expert", scatter_dimension=0, tiled=False
        ).astype(F32)
    half = blocks[0].shape[0] // 2
    other = [swap(blocks[j], 1, "expert") for j in (6 + 1, 2 + 1, 4 + 1, 1)]
    six = (blocks[6].astype(F32) + other[0].astype(F32)).astype(BF)
    two = blocks[2].astype(F32) + other[1].astype(F32)
    four = blocks[4].astype(F32) + other[2].astype(F32)
    six_a = swap(six[:half], 2, "expert")
    six_b = swap(six[half:], 4, "expert")
    two_a = swap(two[:half].astype(BF), 2, "expert")
    four_b = swap(four[half:].astype(BF), 4, "expert")
    four_a = swap((four[:half] + six_a.astype(F32)).astype(BF), 4, "expert")
    two_b = swap((two[half:] + six_b.astype(F32)).astype(BF), 2, "expert")
    mine = blocks[0].astype(F32) + other[3].astype(F32)
    return jnp.concatenate(
        [
            mine[:half] + two_a.astype(F32) + four_a.astype(F32),
            mine[half:] + two_b.astype(F32) + four_b.astype(F32),
        ]
    )


def split_blocks(rows):
    count = lax.axis_size("expert")
    size = rows.shape[0] // count
    return [rows[i * size : (i + 1) * size] for i in range(count)]


def exchange(blocks):
    if not quick_expert():
        swapped = lax.all_to_all(jnp.stack(blocks), "expert", split_axis=0, concat_axis=0)
        return [swapped[i] for i in range(len(blocks))]
    return [blocks[0]] + [swap(blocks[k], k, "expert") for k in range(1, 8)]


def gather_shards(shard):
    if not quick_dp():
        gathered = lax.all_gather(shard, "dp")
        return [gathered[i] for i in range(lax.axis_size("dp"))]
    below = turn(shard, 1)
    above = turn(shard, -1)
    far = turn(below, 1)
    return [shard, below, far, above]


def shard_slot(shard_index):
    if quick_dp():
        return (lax.axis_index("dp") - shard_index) % 4
    return shard_index


def slot_shards():
    places = jnp.arange(lax.axis_size("dp"))
    if quick_dp():
        return (lax.axis_index("dp") - places) % 4
    return places


def sum_shards(parts):
    if not quick_dp():
        return lax.psum_scatter(
            jnp.stack(parts), "dp", scatter_dimension=0, tiled=False
        ).astype(F32)
    own, above_by_three, two, above = parts
    far = turn(two, 1)
    back = turn(above_by_three, -1)
    near = turn((above.astype(F32) + far.astype(F32)).astype(BF), 1)
    return own.astype(F32) + near.astype(F32) + back.astype(F32)


def sum_everywhere(array):
    for axis in ("expert", "dp"):
        bits = 1
        while bits < lax.axis_size(axis):
            array = array + swap(array, bits, axis)
            bits *= 2
    return array


def params():
    return pltpu.CompilerParams(
        dimension_semantics=("arbitrary",), vmem_limit_bytes=VMEM_BYTES
    )


def pair_scores(query, keys, key_place, query_place):
    scores = dot_nt(keys, query)
    return jnp.where(key_place <= query_place, scores, MASKED)


def attend_kernel(q_ref, k_ref, v_ref, kp_ref, qp_ref, mixed_ref, lse_ref):
    step = pl.program_id(0)
    keys, values = k_ref[...], v_ref[...]
    query = q_ref[...]
    lanes = lax.broadcasted_iota(jnp.int32, query.shape, 1)
    head_dim = query.shape[1] // 2
    scale = head_dim ** (-0.5)
    mixed = None
    for part in range(2):
        here = (lanes // head_dim) == part
        masked_query = jnp.where(here, query * scale, 0).astype(BF)
        scores = pair_scores(masked_query, keys, kp_ref[...], qp_ref[...])
        top = jnp.max(scores, axis=0, keepdims=True)
        weights = jnp.exp(scores - top)
        total = jnp.sum(weights, axis=0, keepdims=True)
        out = dot_tn(values, weights.astype(BF)) / total
        out = jnp.transpose(out)
        mixed = out if part == 0 else jnp.where(here, out, mixed)
        lse_ref[pl.ds(2 * step + part, 1), :] = top + jnp.log(total)
    mixed_ref[...] = mixed.astype(BF)


def attend(queries, keys, values, key_place, query_place):
    local, width = queries.shape
    group = keys.shape[0]
    pair = 2 * (width // HEADS)
    steps = HEADS // 2
    return pl.pallas_call(
        attend_kernel,
        grid=(steps,),
        in_specs=[
            pl.BlockSpec((local, pair), lambda i: (0, i)),
            pl.BlockSpec((group, pair), lambda i: (0, i)),
            pl.BlockSpec((group, pair), lambda i: (0, i)),
            pl.BlockSpec((group, 1), lambda i: (0, 0)),
            pl.BlockSpec((1, local), lambda i: (0, 0)),
        ],
        out_specs=[
            pl.BlockSpec((local, pair), lambda i: (0, i)),
            pl.BlockSpec((HEADS, local), lambda i: (0, 0)),
        ],
        out_shape=[
            jax.ShapeDtypeStruct((local, width), BF),
            jax.ShapeDtypeStruct((HEADS, local), F32),
        ],
        compiler_params=params(),
        cost_estimate=pl.CostEstimate(
            flops=4 * local * group * width * 4,
            bytes_accessed=4 * group * width,
            transcendentals=HEADS * local * group,
        ),
        name="attend",
    )(queries, keys, values, key_place, query_place)


def attend_back_kernel(
    q_ref, k_ref, v_ref, do_ref, o_ref, lse_ref, kp_ref, qp_ref, dq_ref, dk_ref, dv_ref
):
    step = pl.program_id(0)
    keys, values = k_ref[...], v_ref[...]
    query, grad_out = q_ref[...], do_ref[...]
    lanes = lax.broadcasted_iota(jnp.int32, query.shape, 1)
    head_dim = query.shape[1] // 2
    scale = head_dim ** (-0.5)
    product = jnp.transpose(grad_out.astype(F32) * o_ref[...].astype(F32))
    grad_query = grad_keys = grad_values = None
    for part in range(2):
        here = (lanes // head_dim) == part
        masked_query = jnp.where(here, query * scale, 0).astype(BF)
        masked_grad = jnp.where(here, grad_out, 0).astype(BF)
        scores = pair_scores(masked_query, keys, kp_ref[...], qp_ref[...])
        weights = jnp.exp(scores - lse_ref[pl.ds(2 * step + part, 1), :])
        delta = jnp.sum(
            product[part * head_dim : (part + 1) * head_dim], axis=0, keepdims=True
        )
        grad_weights = dot_nt(values, masked_grad)
        grad_scores = (weights * (grad_weights - delta)).astype(BF)
        dq = jnp.transpose(dot_tn(keys, grad_scores)) * scale
        dk = dot_nn(grad_scores, masked_query)
        dv = dot_nn(weights.astype(BF), masked_grad)
        if part == 0:
            grad_query, grad_keys, grad_values = dq, dk, dv
        else:
            grad_query = jnp.where(here, dq, grad_query)
            grad_keys, grad_values = grad_keys + dk, grad_values + dv
    dq_ref[...] = grad_query.astype(BF)
    dk_ref[...] = grad_keys.astype(BF)
    dv_ref[...] = grad_values.astype(BF)


def attend_back(queries, keys, values, grad_out, mixed, lse, key_place, query_place):
    local, width = queries.shape
    group = keys.shape[0]
    pair = 2 * (width // HEADS)
    steps = HEADS // 2
    rows = pl.BlockSpec((local, pair), lambda i: (0, i))
    cols = pl.BlockSpec((group, pair), lambda i: (0, i))
    return pl.pallas_call(
        attend_back_kernel,
        grid=(steps,),
        in_specs=[
            rows,
            cols,
            cols,
            rows,
            rows,
            pl.BlockSpec((HEADS, local), lambda i: (0, 0)),
            pl.BlockSpec((group, 1), lambda i: (0, 0)),
            pl.BlockSpec((1, local), lambda i: (0, 0)),
        ],
        out_specs=[rows, cols, cols],
        out_shape=[
            jax.ShapeDtypeStruct((local, width), BF),
            jax.ShapeDtypeStruct((group, width), BF),
            jax.ShapeDtypeStruct((group, width), BF),
        ],
        compiler_params=params(),
        cost_estimate=pl.CostEstimate(
            flops=10 * local * group * width * 4,
            bytes_accessed=8 * group * width,
            transcendentals=HEADS * local * group,
        ),
        name="attend_back",
    )(queries, keys, values, grad_out, mixed, lse, key_place, query_place)


def head_kernel(count, rows_ref, place_ref, *refs):
    heads, exps, stats_ref = refs[:count], refs[count : 2 * count], refs[2 * count]
    rows, place = rows_ref[...], place_ref[...]
    depth = heads[0].shape[0]
    scores = [dot_nt(head[...], rows) for head in heads]
    iota = lax.broadcasted_iota(jnp.int32, scores[0].shape, 0)
    top = functools.reduce(jnp.maximum, [jnp.max(s, axis=0, keepdims=True) for s in scores])
    total = picked = jnp.zeros_like(top)
    for k in range(count):
        weights = jnp.exp(scores[k] - top)
        total = total + jnp.sum(weights, axis=0, keepdims=True)
        chosen = jnp.where(iota == place - k * depth, scores[k], 0.0)
        picked = picked + jnp.sum(chosen, axis=0, keepdims=True)
        exps[k][...] = weights.astype(BF)
    stats_ref[0:1, :] = top
    stats_ref[1:2, :] = total
    stats_ref[2:3, :] = picked
    stats_ref[3:8, :] = jnp.zeros((5, top.shape[1]), F32)


def head_forward(rows, place, heads):
    group, width = rows.shape
    count, depth = len(heads), heads[0].shape[0]
    block = min(256, group)
    whole = pl.BlockSpec((depth, width), lambda i: (0, 0))
    cols = pl.BlockSpec((depth, block), lambda i: (0, i))
    results = pl.pallas_call(
        functools.partial(head_kernel, count),
        grid=(group // block,),
        in_specs=[
            pl.BlockSpec((block, width), lambda i: (i, 0)),
            pl.BlockSpec((1, block), lambda i: (0, i)),
        ]
        + [whole] * count,
        out_specs=[cols] * count + [pl.BlockSpec((8, block), lambda i: (0, i))],
        out_shape=[jax.ShapeDtypeStruct((depth, group), BF)] * count
        + [jax.ShapeDtypeStruct((8, group), F32)],
        compiler_params=params(),
        cost_estimate=pl.CostEstimate(
            flops=2 * group * width * depth * count,
            bytes_accessed=2 * count * depth * (group + width),
            transcendentals=group * depth * count,
        ),
        name="head_forward",
    )(rows, place, *heads)
    return results[:count], results[count]


def logit_grads(exps, coef_ref, place, offset):
    grads = exps.astype(F32) * coef_ref[0:1, :]
    iota = lax.broadcasted_iota(jnp.int32, grads.shape, 0)
    return (grads - jnp.where(iota == place - offset, coef_ref[1:2, :], 0.0)).astype(BF)


def head_rows_kernel(count, coef_ref, place_ref, *refs):
    heads, exps, out_ref = refs[:count], refs[count : 2 * count], refs[2 * count]
    depth = heads[0].shape[0]
    out = None
    for k in range(count):
        grads = logit_grads(exps[k][...], coef_ref, place_ref[...], k * depth)
        term = dot_tn(grads, heads[k][...])
        out = term if out is None else out + term
    out_ref[...] = out.astype(BF)


def head_rows_back(coef, place, heads, exps):
    depth, width = heads[0].shape
    group = exps[0].shape[1]
    count = len(heads)
    block = min(256, group)
    whole = pl.BlockSpec((depth, width), lambda i: (0, 0))
    cols = pl.BlockSpec((depth, block), lambda i: (0, i))
    return pl.pallas_call(
        functools.partial(head_rows_kernel, count),
        grid=(group // block,),
        in_specs=[
            pl.BlockSpec((2, block), lambda i: (0, i)),
            pl.BlockSpec((1, block), lambda i: (0, i)),
        ]
        + [whole] * count
        + [cols] * count,
        out_specs=pl.BlockSpec((block, width), lambda i: (i, 0)),
        out_shape=jax.ShapeDtypeStruct((group, width), BF),
        compiler_params=params(),
        cost_estimate=pl.CostEstimate(
            flops=2 * group * width * depth * count,
            bytes_accessed=2 * count * depth * (group + width),
            transcendentals=0,
        ),
        name="head_rows_back",
    )(coef, place, *heads, *exps)


def head_weight_kernel(offset, coef_ref, place_ref, exps_ref, rows_ref, out_ref, total):
    step = pl.program_id(0)
    grads = logit_grads(exps_ref[...], coef_ref, place_ref[...], offset)
    term = dot_nn(grads, rows_ref[...])

    @pl.when(step == 0)
    def _():
        total[...] = term

    @pl.when(step > 0)
    def _():
        total[...] += term

    @pl.when(step == pl.num_programs(0) - 1)
    def _():
        out_ref[...] = total[...].astype(BF)


def head_weight_back(coef, place, exps, rows, offset):
    depth, group = exps.shape
    width = rows.shape[1]
    block = min(512, group)
    return pl.pallas_call(
        functools.partial(head_weight_kernel, offset),
        grid=(group // block,),
        in_specs=[
            pl.BlockSpec((2, block), lambda i: (0, i)),
            pl.BlockSpec((1, block), lambda i: (0, i)),
            pl.BlockSpec((depth, block), lambda i: (0, i)),
            pl.BlockSpec((block, width), lambda i: (i, 0)),
        ],
        out_specs=pl.BlockSpec((depth, width), lambda i: (0, 0)),
        out_shape=jax.ShapeDtypeStruct((depth, width), BF),
        scratch_shapes=[pltpu.VMEM((depth, width), F32)],
        compiler_params=params(),
        cost_estimate=pl.CostEstimate(
            flops=2 * group * width * depth,
            bytes_accessed=2 * (depth * group + group * width + depth * width),
            transcendentals=0,
        ),
        name="head_weight_back",
    )(coef, place, exps, rows)


def ranks(hits):
    count, length = hits.shape
    cut = hits.reshape(count, length // 128, 128)
    ones = cut.astype(BF)
    before = (jnp.arange(128)[:, None] < jnp.arange(128)[None, :]).astype(BF)
    inner = lax.dot_general(ones, before, (((2,), (0,)), ((), ())), preferred_element_type=F32)
    sums = jnp.sum(ones.astype(F32), axis=2)
    earlier = jnp.arange(length // 128)[:, None] > jnp.arange(length // 128)[None, :]
    outer = jnp.sum(jnp.where(earlier[None], sums[:, None, :], 0.0), axis=2)
    return jnp.where(cut, inner + outer[..., None], -1.0).reshape(count, length)


def split_high_low(values):
    high = lax.reduce_precision(values, 8, 7)
    return high.astype(BF), (values - high).astype(BF)


def body(
    ids,
    targets,
    loss_mask,
    domain_ids,
    expert_lists,
    tables,
    tables_m,
    tables_v,
    attn,
    attn_m,
    attn_v,
    experts,
    experts_m,
    experts_v,
    router,
    router_m,
    router_v,
    gains,
    gains_m,
    gains_v,
):
    shards = lax.axis_size("expert")
    rows_dp = lax.axis_size("dp")
    member = lax.axis_index("expert")
    batch_row = lax.axis_index("dp")
    group = ids.shape[0]
    local = group // shards
    own = member * local
    width = gains.shape[1]
    slots = expert_lists.shape[3]
    words = tables.shape[1]
    order = block_order()

    attn_b = attn.astype(BF)
    if quick_expert() and quick_dp():
        piece = attn.shape[1] // 2
        cut = attn_b.reshape(8, piece, width)
        mine = lax.dynamic_index_in_dim(cut, member, 0, False)
        attn_parts = jnp.stack([mine] + [turn(mine, k) for k in range(1, 4)])
    table_b = tables[0].astype(BF)
    experts_b = experts[0].astype(BF)
    head_b = tables[1].astype(BF)

    capacity = min(group, 2 * (-(-group // (shards * rows_dp))))
    capacity = -(-capacity // 16) * 16
    ids_dp = jnp.stack([ids] + [turn(ids, k) for k in range(1, rows_dp)])
    first_word = (member * rows_dp + batch_row) * words
    ids_own = ids_dp - first_word
    rank_own = ranks((ids_own >= 0) & (ids_own < words))
    ids_own = ids_own.astype(F32)
    place = jnp.arange(capacity, dtype=F32)
    owners = (batch_row + jnp.arange(rows_dp)) % rows_dp
    ids_from = ids[None, :] - ((member * rows_dp + owners) * words)[:, None]
    rank_from = ranks((ids_from >= 0) & (ids_from < words))
    rank_from = rank_from.reshape(rows_dp, shards, local)[:, order].reshape(rows_dp, group)
    owner_of = ids_dp // words
    owner_hits = owner_of[:, None, :] == jnp.arange(shards * rows_dp)[None, :, None]
    most = jnp.max(jnp.sum(owner_hits.astype(F32), axis=2)).astype(jnp.int32)
    rounds = (most + capacity - 1) // capacity

    def own_select(turn_no):
        chosen = rank_own[:, None, :] == (place + turn_no * capacity)[None, :, None]
        at = jnp.sum(jnp.where(chosen, ids_own[:, None, :] + 1.0, 0.0), axis=2) - 1.0
        at = at.reshape(-1)[:, None]
        return (at == jnp.arange(words, dtype=F32)[None, :]).astype(BF)

    def from_select(turn_no):
        at = (place + turn_no * capacity)[None, None, :]
        chosen = rank_from[:, :, None] == at
        return jnp.transpose(chosen, (1, 0, 2)).reshape(group, -1).astype(BF)

    def look_up(turn_no, select_own, select_from):
        found = dot_nn(select_own, table_b).astype(BF).reshape(rows_dp, capacity, width)
        arrived = [found[0]] + [turn(found[k], -k) for k in range(1, rows_dp)]
        return dot_nn(select_from, jnp.concatenate(arrived)).astype(BF)

    def spread(turn_no, grads, select_own, select_from):
        chosen = dot_tn(select_from, grads).astype(BF).reshape(rows_dp, capacity, width)
        arrived = [chosen[0]] + [turn(chosen[k], k) for k in range(1, rows_dp)]
        return dot_tn(select_own, jnp.concatenate(arrived))

    select_own = own_select(0)
    select_from = from_select(0)
    looked = look_up(0, select_own, select_from)
    _, looked = lax.while_loop(
        lambda state: state[0] < rounds,
        lambda state: (
            state[0] + 1,
            state[1]
            + look_up(
                state[0],
                own_select(state[0].astype(F32)),
                from_select(state[0].astype(F32)),
            ),
        ),
        (jnp.int32(1), looked),
    )
    expert_shards = gather_shards(experts_b)
    head_shards = gather_shards(head_b)
    if quick_expert() and quick_dp():
        attn_blocks = gather_blocks(attn_parts.reshape(4 * piece, width))
        attn_blocks = jnp.stack(attn_blocks)[order].reshape(4, 2, 4, piece, width)
        attn_full = jnp.transpose(attn_blocks[:, :, slot_shards()], (0, 2, 1, 3, 4))
        attn_full = attn_full.reshape(4, width, width)
    else:
        attn_full = lax.all_gather(attn_b, "dp", axis=1, tiled=True)
    embedded = sum_blocks(split_blocks(looked))
    router_b = router.astype(BF)

    normed_ab = normed(embedded, gains[0]).astype(BF)
    normed_all = gather_rows(normed_ab)
    queries = dot_nn(normed_ab, attn_full[0]).astype(BF)
    keys = dot_nn(normed_all, attn_full[1]).astype(BF)
    values = dot_nn(normed_all, attn_full[2]).astype(BF)
    token_place = (order[:, None] * local + jnp.arange(local)[None, :]).reshape(-1)
    seq_start = own // SEQ * SEQ
    key_place = jnp.where(token_place >= seq_start, token_place, group)[:, None]
    query_place = (own + jnp.arange(local))[None, :]
    mixed_b, logsum = attend(queries, keys, values, key_place, query_place)
    resid_one = embedded + dot_nn(mixed_b, attn_full[3])

    normed_bb = normed(resid_one, gains[1]).astype(BF)
    router_logits = dot_nn(normed_bb, router_b)
    gates = jax.nn.softmax(router_logits, axis=-1)
    lists = expert_lists[0, 0][order]
    hot = lists[:, :, None] == jnp.arange(local)[None, None, :]
    hot_b = hot.reshape(-1, local).astype(BF)
    gates_mine = jnp.transpose(gates[:, order])
    gate_table = jnp.where(hot, gates_mine[:, None, :], 0.0)
    slot_gates = jnp.sum(gate_table, axis=2).reshape(-1, 1)
    gate_high, gate_low = split_high_low(gate_table.reshape(-1, local))
    send = dot_nn(hot_b, normed_bb).astype(BF)
    received = jnp.concatenate(exchange(split_blocks(send)))
    pres, hiddens, produced = [], [], None
    for shard in expert_shards:
        pre = dot_nn(received, shard[0])
        hidden = gelu(pre).astype(BF)
        term = dot_nt(hidden, shard[1])
        produced = term if produced is None else produced + term
        pres.append(pre)
        hiddens.append(hidden)
    returned = jnp.concatenate(exchange(split_blocks(produced.astype(BF))))
    mixture = dot_tn(gate_high, returned) + dot_tn(gate_low, returned)
    resid_two = resid_one + mixture
    normed_cb = normed(resid_two, gains[2]).astype(BF)

    rows_all = gather_rows(normed_cb)
    targets_mine = targets.reshape(shards, local)[order].reshape(-1)
    word = targets_mine - member * (rows_dp * words)
    word_hit = (word >= 0) & (word < rows_dp * words)
    word_place = jnp.where(word_hit, shard_slot(word // words) * words + word % words, -1)[None, :]
    exps, stats = head_forward(rows_all, word_place, head_shards)
    stats = stats[:3]
    if quick_expert():
        gathered = [stats]
        for k in range(1, 8):
            other = swap(stats, k, "expert")
            gathered.append(
                jnp.concatenate([other[:, (j ^ k) * local : (j ^ k) * local + local] for j in range(8)], axis=1)
            )
        gathered = jnp.stack(gathered)
    else:
        gathered = lax.all_gather(stats, "expert")
    top = jnp.max(gathered[:, 0], axis=0)
    total = jnp.sum(gathered[:, 1] * jnp.exp(gathered[:, 0] - top[None, :]), axis=0)
    logsum_tok = top + jnp.log(total)
    loss_tok = logsum_tok - jnp.sum(gathered[:, 2], axis=0)
    everything = loss_mask.shape[0]
    domain_of = jnp.take(domain_ids, jnp.arange(everything) // SEQ)
    hits = ((domain_of[:, None] == jnp.arange(NDOM)[None, :]) & (loss_mask[:, None] > 0)).astype(
        F32
    )
    counts = jnp.sum(hits, axis=0)
    domain_weight = 10.0 * (NDOM - jnp.arange(NDOM)).astype(F32) / jnp.maximum(counts, 1.0)
    group_hits = lax.dynamic_slice_in_dim(hits, batch_row * group, group, 0)
    group_hits = group_hits.reshape(shards, local, NDOM)[order].reshape(group, NDOM)
    token_weight = jnp.sum(group_hits * domain_weight[None, :], axis=1)
    own_block = 0 if quick_expert() else member
    own_sums = jnp.sum(
        lax.dynamic_slice_in_dim(group_hits, own_block * local, local, 0)
        * lax.dynamic_slice_in_dim(loss_tok, own_block * local, local, 0)[:, None],
        axis=0,
    )
    coef = jnp.stack([token_weight * jnp.exp(stats[0] - logsum_tok), token_weight])
    grad_rows_c = head_rows_back(coef, word_place, head_shards, exps)
    grad_heads = [
        head_weight_back(coef, word_place, exps[k], rows_all, k * words) for k in range(rows_dp)
    ]
    grad_head = sum_shards(grad_heads)
    grad_normed_c = sum_blocks(split_blocks(grad_rows_c))
    grad_two, grad_gain_c = norm_back(resid_two, gains[2], grad_normed_c)

    two_high, two_low = split_high_low(grad_two)
    grad_slot = dot_nn(hot_b, two_high) + dot_nn(hot_b, two_low)
    grad_gate_slot = jnp.sum(grad_slot * returned.astype(F32), axis=-1)
    grad_produced = jnp.concatenate(
        exchange(split_blocks((grad_slot * slot_gates).astype(BF)))
    )
    grad_experts_parts, grad_sent = [], None
    for shard, pre, hidden in zip(expert_shards, pres, hiddens):
        grad_hidden = dot_nn(grad_produced, shard[1])
        _, gelu_pull = jax.vjp(gelu, pre)
        grad_pre = gelu_pull(grad_hidden)[0].astype(BF)
        grad_down = dot_tn(grad_produced, hidden)
        grad_up = dot_tn(received, grad_pre)
        term = dot_nt(grad_pre, shard[0])
        grad_sent = term if grad_sent is None else grad_sent + term
        grad_experts_parts.append(jnp.stack([grad_up, grad_down]).astype(BF))
    grad_experts = sum_shards(grad_experts_parts)[None]
    grad_back = jnp.concatenate(exchange(split_blocks(grad_sent.astype(BF))))
    grad_normed_b = dot_tn(hot_b, grad_back)
    grad_gates = jnp.sum(
        jnp.where(hot, grad_gate_slot.reshape(shards, slots)[:, :, None], 0.0), axis=1
    )
    grad_gates = jnp.transpose(grad_gates[order])
    _, soft_pull = jax.vjp(lambda logit_rows: jax.nn.softmax(logit_rows, axis=-1), router_logits)
    grad_router_logits = soft_pull(grad_gates)[0].astype(BF)
    grad_router = dot_tn(normed_bb, grad_router_logits)
    grad_normed_b = grad_normed_b + dot_nt(grad_router_logits, router_b)
    normal_back, grad_gain_b = norm_back(resid_one, gains[1], grad_normed_b)
    grad_one = grad_two + normal_back

    grad_branch = grad_one.astype(BF)
    grad_wo = dot_tn(mixed_b, grad_branch)
    grad_mixed = dot_nt(grad_branch, attn_full[3]).astype(BF)
    grad_query, grad_keys, grad_values = attend_back(
        queries, keys, values, grad_mixed, mixed_b, logsum, key_place, query_place
    )
    grad_normed_rows = dot_nt(grad_keys, attn_full[1]) + dot_nt(grad_values, attn_full[2])
    grad_normed_a = sum_blocks(split_blocks(grad_normed_rows.astype(BF)))
    grad_normed_a = grad_normed_a + dot_nt(grad_query, attn_full[0])
    normal_front, grad_gain_a = norm_back(embedded, gains[0], grad_normed_a)
    grad_embedded = (grad_one + normal_front).astype(BF)
    grad_embedded_all = gather_rows(grad_embedded)
    grad_embed = spread(0, grad_embedded_all, select_own, select_from)
    _, grad_embed = lax.while_loop(
        lambda state: state[0] < rounds,
        lambda state: (
            state[0] + 1,
            state[1]
            + spread(
                state[0],
                grad_embedded_all,
                own_select(state[0].astype(F32)),
                from_select(state[0].astype(F32)),
            ),
        ),
        (jnp.int32(1), grad_embed),
    )
    grad_attn = jnp.stack(
        [
            dot_tn(normed_ab, grad_query),
            dot_tn(normed_all, grad_keys),
            dot_tn(normed_all, grad_values),
            grad_wo,
        ]
    ).astype(BF)
    if quick_expert() and quick_dp():
        cut = grad_attn.reshape(4, 4, 2, piece, width)
        cut = jnp.transpose(cut, (0, 2, 1, 3, 4)).reshape(8, 4, piece, width)
        cut = cut[order][:, slot_shards()].reshape(8, 4 * piece, width)
        part = sum_blocks([cut[j] for j in range(8)]).astype(BF)
        part = sum_shards([part[k * piece : (k + 1) * piece] for k in range(4)])
        attn_squares = jnp.sum(part * part)
        back = jnp.stack(gather_blocks(part.astype(BF)))[order]
        grad_attn = back.reshape(4, 2 * piece, width).astype(F32)
    else:
        grad_attn = lax.psum_scatter(grad_attn, "dp", scatter_dimension=1, tiled=True)
        grad_attn = lax.psum(grad_attn, "expert").astype(F32)
        attn_squares = jnp.sum(grad_attn * grad_attn) / shards
    squares = (
        jnp.sum(grad_embed * grad_embed)
        + jnp.sum(grad_head * grad_head)
        + jnp.sum(grad_experts * grad_experts)
        + attn_squares
    )
    small = jnp.concatenate(
        [
            grad_router.reshape(-1),
            grad_gain_a,
            grad_gain_b,
            grad_gain_c,
            own_sums,
            squares[None],
        ]
    )
    small = jnp.pad(small, (0, -small.shape[0] % 1024)).reshape(-1, 128)
    small = sum_everywhere(small).reshape(-1)
    edge = router.size
    grad_router = small[:edge].reshape(router.shape)
    grad_gains = small[edge : edge + 3 * width].reshape(3, width)
    domain_sums = small[edge + 3 * width : edge + 3 * width + NDOM]
    squares = small[edge + 3 * width + NDOM]
    grad_norm = jnp.sqrt(
        squares + jnp.sum(grad_router * grad_router) + jnp.sum(grad_gains * grad_gains)
    )
    factor = jnp.minimum(1.0, CLIP / (grad_norm + 1e-06))
    grad_tables = jnp.stack([grad_embed, grad_head])
    tables_out = adam(tables, grad_tables * factor, tables_m, tables_v, 0.1, 0.01)
    attn_out = adam(attn, grad_attn * factor, attn_m, attn_v, 0.1, 0.01)
    experts_out = adam(experts, grad_experts * factor, experts_m, experts_v, 0.1, 0.01)
    router_out = adam(router, grad_router * factor, router_m, router_v, 0.04, 0.01)
    gains_out = adam(gains, grad_gains * factor, gains_m, gains_v, 0.4, 0.0)
    return (
        domain_sums,
        counts,
        grad_norm,
        *tables_out,
        *attn_out,
        *experts_out,
        *router_out,
        *gains_out,
    )


def solution(mesh):
    table = P(None, ("expert", "dp"), None)
    attn = P(None, "dp", None)
    expert = P("expert", None, None, "dp")
    in_specs = (
        P("dp"),
        P("dp"),
        P(),
        P(),
        P("dp", "expert", None, None),
        *[table] * 3,
        *[attn] * 3,
        *[expert] * 3,
        *[P()] * 6,
    )
    out_specs = (*[P()] * 3, *[table] * 4, *[attn] * 4, *[expert] * 4, *[P()] * 8)
    return jax.shard_map(body, mesh=mesh, in_specs=in_specs, out_specs=out_specs, check_vma=False)
```

```python
import functools

import jax
import jax.numpy as jnp
from jax import lax
from jax.experimental import pallas as pl
from jax.experimental.pallas import tpu as pltpu
from jax.sharding import PartitionSpec as P

HEADS = 12
SEQ = 2048
NDOM = 4
STEP = 10


NORM_EPS = 1e-05
BETA = 0.5
ADAM_EPS = 1e-08
CLIP = 1.0
MASKED = -1e30
BF = jnp.bfloat16
F32 = jnp.float32
VMEM_BYTES = 56 * 1024 * 1024


def normed(values, gain):
    return values * lax.rsqrt(jnp.mean(values * values, axis=-1, keepdims=True) + NORM_EPS) * gain


def norm_back(values, gain, grad):
    _, pull = jax.vjp(normed, values, gain)
    return pull(grad)


def gelu(values):
    return jax.nn.gelu(values, approximate=True)


def adam(weight, grad, first, second, rate, decay):
    first = BETA * first + (1.0 - BETA) * grad
    second = BETA * second + (1.0 - BETA) * grad * grad
    correct = 1.0 - BETA**STEP
    weight = weight - rate * (
        first / correct / (jnp.sqrt(second / correct) + ADAM_EPS) + decay * weight
    )
    return (first, second, weight, weight.astype(BF))


def dot(a, b, contract):
    return lax.dot_general(a, b, ((contract[0], contract[1]), ((), ())), preferred_element_type=F32)


def dot_nn(a, b):
    return dot(a, b, ((1,), (0,)))


def dot_nt(a, b):
    return dot(a, b, ((1,), (1,)))


def dot_tn(a, b):
    return dot(a, b, ((0,), (0,)))


def after(array, earlier):
    return array if earlier is None else lax.optimization_barrier((array, earlier))[0]


def swap(array, bits, axis):
    pairs = [(i, i ^ bits) for i in range(lax.axis_size(axis))]
    return lax.ppermute(array, axis, pairs)


def turn(array, steps):
    count = lax.axis_size("dp")
    return lax.ppermute(array, "dp", [(i, (i + steps) % count) for i in range(count)])


def quick_expert():
    return lax.axis_size("expert") == 8


def quick_dp():
    return lax.axis_size("dp") == 4


def block_order():
    count = lax.axis_size("expert")
    if quick_expert():
        return lax.axis_index("expert") ^ jnp.arange(count)
    return jnp.arange(count)


def gather_pieces(rows):
    count = lax.axis_size("expert")
    if not quick_expert():
        gathered = lax.all_gather(rows, "expert")
        return [(i, 0, gathered[i]) for i in range(count)]
    half = rows.shape[0] // 2
    one, two, four = (swap(rows, bits, "expert") for bits in (1, 2, 4))
    six_a = swap(two[:half], 4, "expert")
    six_b = swap(four[half:], 2, "expert")
    three = swap(two, 1, "expert")
    five = swap(four, 1, "expert")
    seven_a = swap(six_a, 1, "expert")
    seven_b = swap(six_b, 1, "expert")
    return [
        (0, 0, rows),
        (1, 0, one),
        (2, 0, two),
        (3, 0, three),
        (4, 0, four),
        (5, 0, five),
        (6, 0, six_a),
        (6, half, six_b),
        (7, 0, seven_a),
        (7, half, seven_b),
    ]


def gather_rows(rows):
    return jnp.concatenate([piece for _, _, piece in gather_pieces(rows)])


def sum_blocks(blocks, earlier=None):
    if not quick_expert():
        return lax.psum_scatter(
            jnp.stack(blocks), "expert", scatter_dimension=0, tiled=False
        ).astype(F32)
    half = blocks[0].shape[0] // 2
    other = [swap(blocks[j], 1, "expert") for j in (6 + 1, 2 + 1, 4 + 1, 1)]
    other[0] = after(other[0], earlier)
    six = (blocks[6].astype(F32) + other[0].astype(F32)).astype(BF)
    two = blocks[2].astype(F32) + other[1].astype(F32)
    four = blocks[4].astype(F32) + other[2].astype(F32)
    six_a = swap(six[:half], 2, "expert")
    six_b = swap(six[half:], 4, "expert")
    two_a = swap(two[:half].astype(BF), 2, "expert")
    four_b = swap(four[half:].astype(BF), 4, "expert")
    four_a = swap((four[:half] + six_a.astype(F32)).astype(BF), 4, "expert")
    two_b = swap((two[half:] + six_b.astype(F32)).astype(BF), 2, "expert")
    mine = blocks[0].astype(F32) + other[3].astype(F32)
    return jnp.concatenate(
        [
            mine[:half] + two_a.astype(F32) + four_a.astype(F32),
            mine[half:] + two_b.astype(F32) + four_b.astype(F32),
        ]
    )


def split_blocks(rows):
    count = lax.axis_size("expert")
    size = rows.shape[0] // count
    return [rows[i * size : (i + 1) * size] for i in range(count)]


def exchange(blocks):
    if not quick_expert():
        swapped = lax.all_to_all(jnp.stack(blocks), "expert", split_axis=0, concat_axis=0)
        return [swapped[i] for i in range(len(blocks))]
    return [blocks[0]] + [swap(blocks[k], k, "expert") for k in range(1, 8)]


def slot_shards():
    return (lax.axis_index("dp") - jnp.arange(4)) % 4


def sum_turns(parts):
    own, above_by_three, two, above = parts
    far = turn(two, 1)
    back = turn(above_by_three, -1)
    near = turn((above.astype(F32) + far.astype(F32)).astype(BF), 1)
    return own.astype(F32) + near.astype(F32) + back.astype(F32)


def sum_shards(parts):
    return lax.psum_scatter(parts, "dp", scatter_dimension=0, tiled=False).astype(F32)


def sum_everywhere(array):
    if quick_expert() and quick_dp():
        array = array + swap(array, 1, "expert")
        for axis, scale in (("expert", 2), ("dp", 1)):
            one, two, three = (swap(array, scale * k, axis) for k in (1, 2, 3))
            array = (array + one) + (two + three)
        return array
    for axis in ("expert", "dp"):
        bits = 1
        while bits < lax.axis_size(axis):
            array = array + swap(array, bits, axis)
            bits *= 2
    return array


def cost(flops):
    return pl.CostEstimate(flops=flops, bytes_accessed=flops // 500, transcendentals=0)


def params():
    return pltpu.CompilerParams(
        dimension_semantics=("arbitrary",), vmem_limit_bytes=VMEM_BYTES
    )


def pair_scores(query, keys, key_place, query_place):
    scores = dot_nt(keys, query)
    return jnp.where(key_place <= query_place, scores, MASKED)


def attend_kernel(q_ref, k_ref, v_ref, kp_ref, qp_ref, mixed_ref, lse_ref):
    step = pl.program_id(0)
    keys, values = k_ref[...], v_ref[...]
    query = q_ref[...]
    lanes = lax.broadcasted_iota(jnp.int32, query.shape, 1)
    head_dim = query.shape[1] // 2
    scale = head_dim ** (-0.5)
    mixed = None
    for part in range(2):
        here = (lanes // head_dim) == part
        masked_query = jnp.where(here, query * scale, 0).astype(BF)
        scores = pair_scores(masked_query, keys, kp_ref[...], qp_ref[...])
        top = jnp.max(scores, axis=0, keepdims=True)
        weights = jnp.exp(scores - top)
        total = jnp.sum(weights, axis=0, keepdims=True)
        out = dot_tn(values, weights.astype(BF)) / total
        out = jnp.transpose(out)
        mixed = out if part == 0 else jnp.where(here, out, mixed)
        lse_ref[pl.ds(2 * step + part, 1), :] = top + jnp.log(total)
    mixed_ref[...] = mixed.astype(BF)


def attend(queries, keys, values, key_place, query_place):
    local, width = queries.shape
    group = keys.shape[0]
    pair = 2 * (width // HEADS)
    steps = HEADS // 2
    return pl.pallas_call(
        attend_kernel,
        grid=(steps,),
        in_specs=[
            pl.BlockSpec((local, pair), lambda i: (0, i)),
            pl.BlockSpec((group, pair), lambda i: (0, i)),
            pl.BlockSpec((group, pair), lambda i: (0, i)),
            pl.BlockSpec((group, 1), lambda i: (0, 0)),
            pl.BlockSpec((1, local), lambda i: (0, 0)),
        ],
        out_specs=[
            pl.BlockSpec((local, pair), lambda i: (0, i)),
            pl.BlockSpec((HEADS, local), lambda i: (0, 0)),
        ],
        out_shape=[
            jax.ShapeDtypeStruct((local, width), BF),
            jax.ShapeDtypeStruct((HEADS, local), F32),
        ],
        compiler_params=params(),
        cost_estimate=cost(1000),
        name="attend",
    )(queries, keys, values, key_place, query_place)


def attend_back_kernel(
    q_ref, k_ref, v_ref, do_ref, o_ref, lse_ref, kp_ref, qp_ref, dq_ref, dk_ref, dv_ref
):
    step = pl.program_id(0)
    keys, values = k_ref[...], v_ref[...]
    query, grad_out = q_ref[...], do_ref[...]
    lanes = lax.broadcasted_iota(jnp.int32, query.shape, 1)
    head_dim = query.shape[1] // 2
    scale = head_dim ** (-0.5)
    product = jnp.transpose(grad_out.astype(F32) * o_ref[...].astype(F32))
    grad_query = grad_keys = grad_values = None
    for part in range(2):
        here = (lanes // head_dim) == part
        masked_query = jnp.where(here, query * scale, 0).astype(BF)
        masked_grad = jnp.where(here, grad_out, 0).astype(BF)
        scores = pair_scores(masked_query, keys, kp_ref[...], qp_ref[...])
        weights = jnp.exp(scores - lse_ref[pl.ds(2 * step + part, 1), :])
        delta = jnp.sum(
            product[part * head_dim : (part + 1) * head_dim], axis=0, keepdims=True
        )
        grad_weights = dot_nt(values, masked_grad)
        grad_scores = (weights * (grad_weights - delta)).astype(BF)
        dq = jnp.transpose(dot_tn(keys, grad_scores)) * scale
        dk = dot_nn(grad_scores, masked_query)
        dv = dot_nn(weights.astype(BF), masked_grad)
        if part == 0:
            grad_query, grad_keys, grad_values = dq, dk, dv
        else:
            grad_query = jnp.where(here, dq, grad_query)
            grad_keys, grad_values = grad_keys + dk, grad_values + dv
    dq_ref[...] = grad_query.astype(BF)
    dk_ref[...] = grad_keys.astype(BF)
    dv_ref[...] = grad_values.astype(BF)


def attend_back(queries, keys, values, grad_out, mixed, lse, key_place, query_place):
    local, width = queries.shape
    group = keys.shape[0]
    pair = 2 * (width // HEADS)
    steps = HEADS // 2
    rows = pl.BlockSpec((local, pair), lambda i: (0, i))
    cols = pl.BlockSpec((group, pair), lambda i: (0, i))
    return pl.pallas_call(
        attend_back_kernel,
        grid=(steps,),
        in_specs=[
            rows,
            cols,
            cols,
            rows,
            rows,
            pl.BlockSpec((HEADS, local), lambda i: (0, 0)),
            pl.BlockSpec((group, 1), lambda i: (0, 0)),
            pl.BlockSpec((1, local), lambda i: (0, 0)),
        ],
        out_specs=[rows, cols, cols],
        out_shape=[
            jax.ShapeDtypeStruct((local, width), BF),
            jax.ShapeDtypeStruct((group, width), BF),
            jax.ShapeDtypeStruct((group, width), BF),
        ],
        compiler_params=params(),
        cost_estimate=cost(1000),
        name="attend_back",
    )(queries, keys, values, grad_out, mixed, lse, key_place, query_place)


def place_kernel(spots, member_ref, *refs):
    pieces, out_ref = refs[: len(spots)], refs[len(spots)]
    half = out_ref.shape[2] // 2
    for i, (block, row) in enumerate(spots):
        owner = member_ref[0] ^ block
        columns = pl.ds(pl.multiple_of((owner % 2) * half, 128), half)
        out_ref[owner // 2, row : row + pieces[i].shape[0], columns] = pieces[i][...]


def place_halves(member, pieces):
    spots = [(block, row) for block, row, _ in pieces]
    arrays = [array for _, _, array in pieces]
    rows, half = arrays[0].shape
    return pl.pallas_call(
        functools.partial(place_kernel, spots),
        in_specs=[pl.BlockSpec(memory_space=pltpu.SMEM)]
        + [pl.BlockSpec(memory_space=pltpu.VMEM)] * len(arrays),
        out_specs=pl.BlockSpec(memory_space=pltpu.VMEM),
        out_shape=jax.ShapeDtypeStruct((4, rows, 2 * half), arrays[0].dtype),
        compiler_params=pltpu.CompilerParams(vmem_limit_bytes=VMEM_BYTES),
        cost_estimate=cost(1000),
        name="place_halves",
    )(member.reshape(1), *arrays)


def attn_weight_kernel(
    member_ref, x_ref, all_ref, mixed_ref, q_ref, k_ref, v_ref, branch_ref, out_ref
):
    owner = member_ref[0] ^ pl.program_id(0)
    half = out_ref.shape[2]
    columns = pl.ds(pl.multiple_of((owner % 2) * half, 128), half)
    sources = ((x_ref, q_ref), (all_ref, k_ref), (all_ref, v_ref), (mixed_ref, branch_ref))
    for kind, (left, right) in enumerate(sources):

        @pl.when(owner // 2 == kind)
        def _(left=left, right=right):
            out_ref[0] = dot_tn(left[...], right[:, columns]).astype(BF)


def attn_weight_back(member, *arrays):
    width = arrays[0].shape[1]
    return pl.pallas_call(
        attn_weight_kernel,
        grid=(8,),
        in_specs=[pl.BlockSpec(memory_space=pltpu.SMEM)]
        + [pl.BlockSpec(a.shape, lambda i: (0, 0)) for a in arrays],
        out_specs=pl.BlockSpec((1, width, width // 2), lambda i: (i, 0, 0)),
        out_shape=jax.ShapeDtypeStruct((8, width, width // 2), BF),
        compiler_params=params(),
        cost_estimate=cost(4 * (arrays[0].shape[0] + arrays[1].shape[0]) * width * width),
        name="attn_weight_back",
    )(member.reshape(1), *arrays)


def head_kernel(rows_ref, heads_ref, exps_ref, stats_ref):
    rows = rows_ref[...]
    count = heads_ref.shape[0]
    for k in range(count):
        scores = dot_nt(heads_ref[k], rows)
        top = jnp.max(scores, axis=0, keepdims=True)
        weights = jnp.exp(scores - top)
        stats_ref[k : k + 1, :] = top
        stats_ref[count + k : count + k + 1, :] = jnp.sum(weights, axis=0, keepdims=True)
        exps_ref[k] = weights.astype(BF)


def head_forward(rows, heads):
    group, width = rows.shape
    count, depth, _ = heads.shape
    block = min(512, group)
    exps, stats = pl.pallas_call(
        head_kernel,
        grid=(group // block,),
        in_specs=[
            pl.BlockSpec((block, width), lambda i: (i, 0)),
            pl.BlockSpec((count, depth, width), lambda i: (0, 0, 0)),
        ],
        out_specs=[
            pl.BlockSpec((count, depth, block), lambda i: (0, 0, i)),
            pl.BlockSpec((2 * count, block), lambda i: (0, i)),
        ],
        out_shape=[
            jax.ShapeDtypeStruct((count, depth, group), BF),
            jax.ShapeDtypeStruct((2 * count, group), F32),
        ],
        compiler_params=params(),
        cost_estimate=cost(2 * group * width * depth * count),
        name="head_forward",
    )(rows, heads)
    return exps, stats


def chosen_tokens(rank_ref, word_ref, k, turn_no, capacity):
    group = rank_ref.shape[1]
    place = lax.broadcasted_iota(jnp.int32, (capacity, group), 0) + turn_no * capacity
    chosen = rank_ref[k : k + 1, :] == place.astype(F32)
    word = jnp.sum(jnp.where(chosen, word_ref[...] + 1.0, 0.0), axis=1, keepdims=True) - 1.0
    return chosen, word


def word_hots(word, words):
    lanes = lax.broadcasted_iota(jnp.int32, (word.shape[0], words), 1).astype(F32)
    return (word == lanes).astype(BF)


def stats_kernel(
    capacity, rounds_ref, rank_ref, word_ref, heads_ref, rows_ref, sums_ref, out_ref, stats_ref,
    ratio_ref
):
    count, words, _ = heads_ref.shape

    def wanted(turn_no):
        picks, found = [], []
        for k in range(count):
            chosen, word = chosen_tokens(rank_ref, word_ref, k, turn_no, capacity)
            picks.append(jnp.where(chosen, 1.0, 0.0).astype(BF))
            found.append(dot_nn(word_hots(word, words), heads_ref[k]).astype(BF))
        return dot_tn(jnp.concatenate(picks), jnp.concatenate(found))

    out_ref[...] = wanted(0).astype(BF)

    @pl.loop(1, rounds_ref[0])
    def _(turn_no):
        out_ref[...] = (out_ref[...].astype(F32) + wanted(turn_no)).astype(BF)

    product = rows_ref[...].astype(F32) * out_ref[...].astype(F32)
    high = product.astype(BF)
    low = (product - high.astype(F32)).astype(BF)
    ones = jnp.ones((8, product.shape[1]), BF)
    picked = dot_nt(ones, high) + dot_nt(ones, low)
    tops = sums_ref[:count, :]
    top = jnp.max(tops, axis=0, keepdims=True)
    ratio = jnp.exp(tops - top)
    ratio_ref[...] = ratio
    stats_ref[0:1, :] = top
    stats_ref[1:2, :] = jnp.sum(sums_ref[count:, :] * ratio, axis=0, keepdims=True)
    stats_ref[2:3, :] = picked[0:1, :]


def target_kernel(capacity, rounds_ref, rank_ref, word_ref, weight_ref, rows_ref, out_ref):
    count, words, _ = out_ref.shape

    def term(k, turn_no):
        chosen, word = chosen_tokens(rank_ref, word_ref, k, turn_no, capacity)
        weight = jnp.sum(jnp.where(chosen, weight_ref[...], 0.0), axis=1, keepdims=True)
        found = dot_nn(jnp.where(chosen, 1.0, 0.0).astype(BF), rows_ref[...]) * weight
        return dot_tn(word_hots(word, words), found.astype(BF))

    for k in range(count):
        out_ref[k] = term(k, 0).astype(BF)

    @pl.loop(1, rounds_ref[0])
    def _(turn_no):
        for k in range(count):
            out_ref[k] = (out_ref[k].astype(F32) + term(k, turn_no)).astype(BF)


def whole_call(kernel, out_shape, name, *arrays):
    vmem = pl.BlockSpec(memory_space=pltpu.VMEM)
    return pl.pallas_call(
        kernel,
        in_specs=[pl.BlockSpec(memory_space=pltpu.SMEM)] + [vmem] * (len(arrays) - 1),
        out_specs=jax.tree.map(lambda _: vmem, out_shape),
        out_shape=out_shape,
        compiler_params=pltpu.CompilerParams(vmem_limit_bytes=VMEM_BYTES),
        cost_estimate=cost(1000),
        name=name,
    )(*arrays)


def head_rows_kernel(coef_ref, heads_ref, exps_ref, out_ref):
    coef = jnp.transpose(coef_ref[...])
    out = None
    for k in range(heads_ref.shape[0]):
        term = dot_tn(exps_ref[k], heads_ref[k]) * coef[:, k : k + 1]
        out = term if out is None else out + term
    out_ref[...] = out.astype(BF)


def head_rows_back(coef, heads, exps):
    count, depth, width = heads.shape
    group = exps.shape[2]
    block = min(256, group)
    return pl.pallas_call(
        head_rows_kernel,
        grid=(group // block,),
        in_specs=[
            pl.BlockSpec((count, block), lambda i: (0, i)),
            pl.BlockSpec((count, depth, width), lambda i: (0, 0, 0)),
            pl.BlockSpec((count, depth, block), lambda i: (0, 0, i)),
        ],
        out_specs=pl.BlockSpec((block, width), lambda i: (i, 0)),
        out_shape=jax.ShapeDtypeStruct((group, width), BF),
        compiler_params=params(),
        cost_estimate=cost(2 * group * width * depth * count),
        name="head_rows_back",
    )(coef, heads, exps)


def ranks(hits):
    count, length = hits.shape
    cut = hits.reshape(count, length // 128, 128)
    ones = cut.astype(BF)
    before = (jnp.arange(128)[:, None] < jnp.arange(128)[None, :]).astype(BF)
    inner = lax.dot_general(ones, before, (((2,), (0,)), ((), ())), preferred_element_type=F32)
    sums = jnp.sum(ones.astype(F32), axis=2)
    earlier = jnp.arange(length // 128)[:, None] > jnp.arange(length // 128)[None, :]
    outer = jnp.sum(jnp.where(earlier[None], sums[:, None, :], 0.0), axis=2)
    return jnp.where(cut, inner + outer[..., None], -1.0).reshape(count, length)


def split_high_low(values):
    high = lax.reduce_precision(values, 8, 7)
    return high.astype(BF), (values - high).astype(BF)


def body(
    ids,
    targets,
    loss_mask,
    domain_ids,
    expert_lists,
    tables,
    tables_m,
    tables_v,
    attn,
    attn_m,
    attn_v,
    experts,
    experts_m,
    experts_v,
    router,
    router_m,
    router_v,
    gains,
    gains_m,
    gains_v,
):
    shards = lax.axis_size("expert")
    rows_dp = lax.axis_size("dp")
    member = lax.axis_index("expert")
    batch_row = lax.axis_index("dp")
    group = ids.shape[0]
    local = group // shards
    own = member * local
    width = gains.shape[1]
    slots = expert_lists.shape[3]
    words = tables.shape[1]
    order = block_order()

    attn_b = attn.astype(BF)
    if quick_expert() and quick_dp():
        mine = lax.dynamic_slice(
            attn_b,
            (member // 2, 0, (member % 2) * (width // 2)),
            (1, attn.shape[1], width // 2),
        )[0]
        attn_parts = jnp.stack([mine] + [turn(mine, k) for k in range(1, 4)])
        attn_parts = attn_parts[slot_shards()].reshape(width, width // 2)
        attn_pieces = gather_pieces(attn_parts)
    table_b = tables[0].astype(BF)
    experts_b = experts[0].astype(BF)
    head_b = tables[1].astype(BF)

    capacity = min(group, 2 * (-(-group // (shards * rows_dp))))
    capacity = -(-capacity // 16) * 16
    ids_dp = jnp.stack([ids] + [turn(ids, k) for k in range(1, rows_dp)])
    first_word = (member * rows_dp + batch_row) * words
    ids_own = ids_dp - first_word
    rank_own = ranks((ids_own >= 0) & (ids_own < words))
    ids_own = ids_own.astype(F32)
    place = jnp.arange(capacity, dtype=F32)
    owners = (batch_row + jnp.arange(rows_dp)) % rows_dp
    ids_from = ids[None, :] - ((member * rows_dp + owners) * words)[:, None]
    rank_from = ranks((ids_from >= 0) & (ids_from < words))
    rank_from = rank_from.reshape(rows_dp, shards, local)[:, order].reshape(rows_dp, group)
    owner_of = ids_dp // words
    owner_hits = owner_of[:, None, :] == jnp.arange(shards * rows_dp)[None, :, None]
    most = jnp.max(jnp.sum(owner_hits.astype(F32), axis=2)).astype(jnp.int32)
    rounds = (most + capacity - 1) // capacity

    def own_select(turn_no):
        chosen = rank_own[:, None, :] == (place + turn_no * capacity)[None, :, None]
        at = jnp.sum(jnp.where(chosen, ids_own[:, None, :] + 1.0, 0.0), axis=2) - 1.0
        at = at.reshape(-1)[:, None]
        return (at == jnp.arange(words, dtype=F32)[None, :]).astype(BF)

    def from_select(turn_no):
        chosen = rank_from[:, None, :] == (place + turn_no * capacity)[None, :, None]
        return chosen.reshape(-1, group).astype(BF)

    def look_up(select_own):
        found = dot_nn(select_own, table_b).astype(BF).reshape(rows_dp, capacity, width)
        arrived = [found[0]] + [turn(found[k], -k) for k in range(1, rows_dp)]
        return jnp.concatenate(arrived)

    def put(arrived, select_from):
        return dot_tn(select_from, arrived).astype(BF)

    def spread(turn_no, grads, select_own, select_from):
        chosen = dot_nn(select_from, grads).astype(BF).reshape(rows_dp, capacity, width)
        arrived = [chosen[0]] + [turn(chosen[k], k) for k in range(1, rows_dp)]
        return dot_tn(select_own, jnp.concatenate(arrived))

    targets_mine = targets.reshape(shards, local)[order].reshape(-1)
    word = targets_mine - member * (rows_dp * words)
    word_slot = jnp.where((word >= 0) & (word < rows_dp * words), word // words, rows_dp)
    word_row = (word % words).astype(F32)[None, :]
    word_hits = word_slot[None, :] == jnp.arange(rows_dp)[:, None]
    word_rank = ranks(word_hits)
    word_most = jnp.max(jnp.sum(word_hits.astype(F32), axis=1)).astype(jnp.int32)
    word_rounds = ((word_most + capacity - 1) // capacity).reshape(1)

    def token_weights():
        everything = loss_mask.shape[0]
        domain_of = jnp.take(domain_ids, jnp.arange(everything) // SEQ)
        hits = ((domain_of[:, None] == jnp.arange(NDOM)[None, :]) & (loss_mask[:, None] > 0)).astype(
            F32
        )
        counts = jnp.sum(hits, axis=0)
        domain_weight = 10.0 * (NDOM - jnp.arange(NDOM)).astype(F32) / jnp.maximum(counts, 1.0)
        group_hits = lax.dynamic_slice_in_dim(hits, batch_row * group, group, 0)
        group_hits = group_hits.reshape(shards, local, NDOM)[order].reshape(group, NDOM)
        token_weight = jnp.sum(group_hits * domain_weight[None, :], axis=1)
        return token_weight, group_hits, counts

    token_weight, group_hits, counts = token_weights()
    lists = expert_lists[0, 0][order]
    hot = lists[:, :, None] == jnp.arange(local)[None, None, :]
    hot_b = hot.reshape(-1, local).astype(BF)
    select_own = own_select(0)
    select_from = from_select(0)
    quick = quick_expert() and quick_dp()
    arrived = look_up(select_own)
    expert_shards = lax.all_gather(experts_b, "dp")
    looked = put(arrived, select_from)
    _, looked = lax.while_loop(
        lambda state: state[0] < rounds,
        lambda state: (
            state[0] + 1,
            state[1]
            + put(
                look_up(own_select(state[0].astype(F32))),
                from_select(state[0].astype(F32)),
            ),
        ),
        (jnp.int32(1), looked),
    )
    if quick_expert() and quick_dp():
        attn_full = place_halves(member, attn_pieces)
    else:
        attn_full = lax.all_gather(attn_b, "dp", axis=1, tiled=True)
    embedded = sum_blocks(split_blocks(looked))
    router_b = router.astype(BF)

    normed_ab = normed(embedded, gains[0]).astype(BF)
    normed_all = gather_rows(normed_ab)
    queries = dot_nn(normed_ab, attn_full[0]).astype(BF)
    keys = dot_nn(normed_all, attn_full[1]).astype(BF)
    values = dot_nn(normed_all, attn_full[2]).astype(BF)
    token_place = (order[:, None] * local + jnp.arange(local)[None, :]).reshape(-1)
    seq_start = own // SEQ * SEQ
    key_place = jnp.where(token_place >= seq_start, token_place, group)[:, None]
    query_place = (own + jnp.arange(local))[None, :]
    mixed_b, logsum = attend(queries, keys, values, key_place, query_place)
    resid_one = embedded + dot_nn(mixed_b, attn_full[3])

    normed_bb = normed(resid_one, gains[1]).astype(BF)
    router_logits = dot_nn(normed_bb, router_b)
    gates = jax.nn.softmax(router_logits, axis=-1)
    gates_mine = jnp.transpose(gates[:, order])
    gate_table = jnp.where(hot, gates_mine[:, None, :], 0.0)
    slot_gates = jnp.sum(gate_table, axis=2).reshape(-1, 1)
    gate_high, gate_low = split_high_low(gate_table.reshape(-1, local))
    send = dot_nn(hot_b, normed_bb).astype(BF)
    received = jnp.concatenate(exchange(split_blocks(send)))
    head_shards = lax.all_gather(after(head_b, expert_shards), "dp")
    pres, hiddens, produced = [], [], None
    for shard in expert_shards:
        pre = dot_nn(received, shard[0])
        hidden = gelu(pre).astype(BF)
        term = dot_nt(hidden, shard[1])
        produced = term if produced is None else produced + term
        pres.append(pre)
        hiddens.append(hidden)
    returned = jnp.concatenate(exchange(split_blocks(produced.astype(BF))))
    mixture = dot_tn(gate_high, returned) + dot_tn(gate_low, returned)
    resid_two = resid_one + mixture
    normed_cb = normed(resid_two, gains[2]).astype(BF)

    rows_all = gather_rows(normed_cb)
    target_terms = whole_call(
        functools.partial(target_kernel, capacity),
        jax.ShapeDtypeStruct((rows_dp, words, width), BF),
        "target_terms",
        word_rounds,
        word_rank,
        word_row,
        token_weight[None, :],
        rows_all,
    )
    exps, head_stats = head_forward(rows_all, head_shards)
    tops = head_stats[:rows_dp]
    wanted, stats, ratios = whole_call(
        functools.partial(stats_kernel, capacity),
        (
            jax.ShapeDtypeStruct((group, width), BF),
            jax.ShapeDtypeStruct((3, group), F32),
            jax.ShapeDtypeStruct((rows_dp, group), F32),
        ),
        "target_stats",
        word_rounds,
        word_rank,
        word_row,
        head_shards,
        rows_all,
        head_stats,
    )
    top_here = stats[0]
    if quick_expert():
        gathered = [stats]
        for k in range(1, 8):
            other = swap(stats, k, "expert")
            gathered.append(
                jnp.concatenate([other[:, (j ^ k) * local : (j ^ k) * local + local] for j in range(8)], axis=1)
            )
        gathered = jnp.stack(gathered)
    else:
        gathered = lax.all_gather(stats, "expert")
    top = jnp.max(gathered[:, 0], axis=0)
    total = jnp.sum(gathered[:, 1] * jnp.exp(gathered[:, 0] - top[None, :]), axis=0)
    logsum_tok = top + jnp.log(total)
    loss_tok = logsum_tok - jnp.sum(gathered[:, 2], axis=0)
    own_block = 0 if quick_expert() else member
    own_sums = jnp.sum(
        lax.dynamic_slice_in_dim(group_hits, own_block * local, local, 0)
        * lax.dynamic_slice_in_dim(loss_tok, own_block * local, local, 0)[:, None],
        axis=0,
    )
    spread_rows = head_rows_back(ratios, head_shards, exps)
    scales = token_weight[None, :] * jnp.exp(tops - logsum_tok[None, :])
    scale_here = token_weight * jnp.exp(top_here - logsum_tok)
    grad_heads = [
        (
            dot_nn(exps[k], (rows_all.astype(F32) * scales[k][:, None]).astype(BF))
            - target_terms[k].astype(F32)
        ).astype(BF)
        for k in range(rows_dp)
    ]
    grad_head = sum_shards(jnp.stack(grad_heads))
    grad_rows_c = (
        spread_rows.astype(F32) * scale_here[:, None]
        - wanted.astype(F32) * token_weight[:, None]
    ).astype(BF)
    grad_normed_c = sum_blocks(split_blocks(grad_rows_c))
    grad_two, grad_gain_c = norm_back(resid_two, gains[2], grad_normed_c)

    two_high, two_low = split_high_low(grad_two)
    grad_slot = dot_nn(hot_b, two_high) + dot_nn(hot_b, two_low)
    grad_gate_slot = jnp.sum(grad_slot * returned.astype(F32), axis=-1)
    grad_produced = jnp.concatenate(
        exchange(split_blocks((grad_slot * slot_gates).astype(BF)))
    )
    grad_parts, grad_sent = [], None
    for k in range(rows_dp):
        grad_hidden = dot_nn(grad_produced, expert_shards[k, 1])
        _, gelu_pull = jax.vjp(gelu, pres[k])
        grad_pre = gelu_pull(grad_hidden)[0].astype(BF)
        grad_parts.append(dot_tn(received, grad_pre).astype(BF))
        grad_parts.append(dot_tn(grad_produced, hiddens[k]).astype(BF))
        term = dot_nt(grad_pre, expert_shards[k, 0])
        grad_sent = term if grad_sent is None else grad_sent + term
    grad_parts = jnp.stack(grad_parts).reshape(rows_dp, 2, width, -1)
    grad_experts = sum_shards(grad_parts)[None]
    grad_back = jnp.concatenate(exchange(split_blocks(grad_sent.astype(BF))))
    grad_normed_b = dot_tn(hot_b, grad_back)
    grad_gates = jnp.sum(
        jnp.where(hot, grad_gate_slot.reshape(shards, slots)[:, :, None], 0.0), axis=1
    )
    grad_gates = jnp.transpose(grad_gates[order])
    _, soft_pull = jax.vjp(lambda logit_rows: jax.nn.softmax(logit_rows, axis=-1), router_logits)
    grad_router_logits = soft_pull(grad_gates)[0].astype(BF)
    grad_router = dot_tn(normed_bb, grad_router_logits)
    grad_normed_b = grad_normed_b + dot_nt(grad_router_logits, router_b)
    normal_back, grad_gain_b = norm_back(resid_one, gains[1], grad_normed_b)
    grad_one = grad_two + normal_back

    grad_branch = grad_one.astype(BF)
    grad_mixed = dot_nt(grad_branch, attn_full[3]).astype(BF)
    grad_query, grad_keys, grad_values = attend_back(
        queries, keys, values, grad_mixed, mixed_b, logsum, key_place, query_place
    )
    grad_normed_rows = dot_nt(grad_keys, attn_full[1]) + dot_nt(grad_values, attn_full[2])
    grad_normed_a = sum_blocks(split_blocks(grad_normed_rows.astype(BF)))
    grad_normed_a = grad_normed_a + dot_nt(grad_query, attn_full[0])
    normal_front, grad_gain_a = norm_back(embedded, gains[0], grad_normed_a)
    grad_embedded = (grad_one + normal_front).astype(BF)
    grad_embedded_all = gather_rows(grad_embedded)
    grad_embed = spread(0, grad_embedded_all, select_own, select_from)
    _, grad_embed = lax.while_loop(
        lambda state: state[0] < rounds,
        lambda state: (
            state[0] + 1,
            state[1]
            + spread(
                state[0],
                grad_embedded_all,
                own_select(state[0].astype(F32)),
                from_select(state[0].astype(F32)),
            ),
        ),
        (jnp.int32(1), grad_embed),
    )
    if quick_expert() and quick_dp():
        blocks = attn_weight_back(
            member,
            normed_ab,
            normed_all,
            mixed_b,
            grad_query,
            grad_keys,
            grad_values,
            grad_branch,
        )
        part = sum_blocks([blocks[j] for j in range(8)]).astype(BF)
        part = part.reshape(4, width // 4, width // 2)[slot_shards()]
        part = sum_turns([part[k] for k in range(4)])
        attn_squares = jnp.sum(part * part)
        grad_attn = place_halves(member, gather_pieces(part.astype(BF))).astype(F32)
    else:
        grad_attn = jnp.stack(
            [
                dot_tn(normed_ab, grad_query),
                dot_tn(normed_all, grad_keys),
                dot_tn(normed_all, grad_values),
                dot_tn(mixed_b, grad_branch),
            ]
        ).astype(BF)
        grad_attn = lax.psum_scatter(grad_attn, "dp", scatter_dimension=1, tiled=True)
        grad_attn = lax.psum(grad_attn, "expert").astype(F32)
        attn_squares = jnp.sum(grad_attn * grad_attn) / shards
    squares = (
        jnp.sum(grad_embed * grad_embed)
        + jnp.sum(grad_head * grad_head)
        + jnp.sum(grad_experts * grad_experts)
        + attn_squares
    )
    small = jnp.concatenate(
        [
            grad_router.reshape(-1),
            grad_gain_a,
            grad_gain_b,
            grad_gain_c,
            own_sums,
            squares[None],
        ]
    )
    small = jnp.pad(small, (0, -small.shape[0] % 1024)).reshape(-1, 128)
    small = sum_everywhere(small).reshape(-1)
    edge = router.size
    grad_router = small[:edge].reshape(router.shape)
    grad_gains = small[edge : edge + 3 * width].reshape(3, width)
    domain_sums = small[edge + 3 * width : edge + 3 * width + NDOM]
    squares = small[edge + 3 * width + NDOM]
    grad_norm = jnp.sqrt(
        squares + jnp.sum(grad_router * grad_router) + jnp.sum(grad_gains * grad_gains)
    )
    factor = jnp.minimum(1.0, CLIP / (grad_norm + 1e-06))
    grad_tables = jnp.stack([grad_embed, grad_head])
    tables_out = adam(tables, grad_tables * factor, tables_m, tables_v, 0.1, 0.01)
    attn_out = adam(attn, grad_attn * factor, attn_m, attn_v, 0.1, 0.01)
    experts_out = adam(experts, grad_experts * factor, experts_m, experts_v, 0.1, 0.01)
    router_out = adam(router, grad_router * factor, router_m, router_v, 0.04, 0.01)
    gains_out = adam(gains, grad_gains * factor, gains_m, gains_v, 0.4, 0.0)
    return (
        domain_sums,
        counts,
        grad_norm,
        *tables_out,
        *attn_out,
        *experts_out,
        *router_out,
        *gains_out,
    )


def solution(mesh):
    table = P(None, ("expert", "dp"), None)
    attn = P(None, "dp", None)
    expert = P("expert", None, None, "dp")
    in_specs = (
        P("dp"),
        P("dp"),
        P(),
        P(),
        P("dp", "expert", None, None),
        *[table] * 3,
        *[attn] * 3,
        *[expert] * 3,
        *[P()] * 6,
    )
    out_specs = (*[P()] * 3, *[table] * 4, *[attn] * 4, *[expert] * 4, *[P()] * 8)
    return jax.shard_map(body, mesh=mesh, in_specs=in_specs, out_specs=out_specs, check_vma=False)
```

```python
import functools

import jax
import jax.numpy as jnp
from jax import lax
from jax.experimental import pallas as pl
from jax.experimental.pallas import tpu as pltpu
from jax.sharding import PartitionSpec as P

HEADS = 12
SEQ = 2048
NDOM = 4
STEP = 10


NORM_EPS = 1e-05
BETA = 0.5
ADAM_EPS = 1e-08
CLIP = 1.0
MASKED = -1e30
BF = jnp.bfloat16
F32 = jnp.float32
VMEM_BYTES = 56 * 1024 * 1024


def normed(values, gain):
    return values * lax.rsqrt(jnp.mean(values * values, axis=-1, keepdims=True) + NORM_EPS) * gain


def norm_back(values, gain, grad):
    _, pull = jax.vjp(normed, values, gain)
    return pull(grad)


def gelu(values):
    return jax.nn.gelu(values, approximate=True)


def adam(weight, grad, first, second, rate, decay):
    first = BETA * first + (1.0 - BETA) * grad
    second = BETA * second + (1.0 - BETA) * grad * grad
    correct = 1.0 - BETA**STEP
    weight = weight - rate * (
        first / correct / (jnp.sqrt(second / correct) + ADAM_EPS) + decay * weight
    )
    return (first, second, weight, weight.astype(BF))


def dot(a, b, contract):
    return lax.dot_general(a, b, ((contract[0], contract[1]), ((), ())), preferred_element_type=F32)


def dot_nn(a, b):
    return dot(a, b, ((1,), (0,)))


def dot_nt(a, b):
    return dot(a, b, ((1,), (1,)))


def dot_tn(a, b):
    return dot(a, b, ((0,), (0,)))


def after(array, earlier):
    return array if earlier is None else lax.optimization_barrier((array, earlier))[0]


def swap(array, bits, axis):
    pairs = [(i, i ^ bits) for i in range(lax.axis_size(axis))]
    return lax.ppermute(array, axis, pairs)


def turn(array, steps):
    count = lax.axis_size("dp")
    return lax.ppermute(array, "dp", [(i, (i + steps) % count) for i in range(count)])


def quick_expert():
    return lax.axis_size("expert") == 8


def quick_dp():
    return lax.axis_size("dp") == 4


def block_order():
    count = lax.axis_size("expert")
    if quick_expert():
        return lax.axis_index("expert") ^ jnp.arange(count)
    return jnp.arange(count)


def gather_pieces(rows):
    count = lax.axis_size("expert")
    if not quick_expert():
        gathered = lax.all_gather(rows, "expert")
        return [(i, 0, gathered[i]) for i in range(count)]
    half = rows.shape[0] // 2
    one, two, four = (swap(rows, bits, "expert") for bits in (1, 2, 4))
    six_a = swap(two[:half], 4, "expert")
    six_b = swap(four[half:], 2, "expert")
    three = swap(two, 1, "expert")
    five = swap(four, 1, "expert")
    seven_a = swap(six_a, 1, "expert")
    seven_b = swap(six_b, 1, "expert")
    return [
        (0, 0, rows),
        (1, 0, one),
        (2, 0, two),
        (3, 0, three),
        (4, 0, four),
        (5, 0, five),
        (6, 0, six_a),
        (6, half, six_b),
        (7, 0, seven_a),
        (7, half, seven_b),
    ]


def gather_rows(rows):
    return jnp.concatenate([piece for _, _, piece in gather_pieces(rows)])


def sum_blocks(blocks, firsts=None):
    if not quick_expert():
        return lax.psum_scatter(
            jnp.stack(blocks), "expert", scatter_dimension=0, tiled=False
        ).astype(F32)
    half = blocks[0].shape[0] // 2
    width = blocks[0].shape[1]
    other = [swap(blocks[j], 1, "expert") for j in (7, 3, 5, 1)]
    piece, piece_f = (jax.ShapeDtypeStruct((half, width), t) for t in (BF, F32))
    six_a, six_b, two_a, four_b, two_f, four_f, mine = whole_call(
        first_sum_kernel,
        [piece] * 4 + [piece_f] * 2 + [jax.ShapeDtypeStruct((2 * half, width), F32)],
        "first_sum",
        *[blocks[j] for j in (6, 2, 4, 0)],
        *other,
    )
    if firsts is not None:
        firsts.append((six_a, two_a))
    six_a = swap(six_a, 2, "expert")
    six_b = swap(six_b, 4, "expert")
    two_a = swap(two_a, 2, "expert")
    four_b = swap(four_b, 4, "expert")
    four_a = swap((four_f + six_a.astype(F32)).astype(BF), 4, "expert")
    two_b = swap((two_f + six_b.astype(F32)).astype(BF), 2, "expert")
    return mine + jnp.concatenate(
        [
            two_a.astype(F32) + four_a.astype(F32),
            two_b.astype(F32) + four_b.astype(F32),
        ]
    )


def split_blocks(rows):
    count = lax.axis_size("expert")
    size = rows.shape[0] // count
    return [rows[i * size : (i + 1) * size] for i in range(count)]


def exchange(blocks):
    if not quick_expert():
        swapped = lax.all_to_all(jnp.stack(blocks), "expert", split_axis=0, concat_axis=0)
        return [swapped[i] for i in range(len(blocks))]
    return [blocks[0]] + [swap(blocks[k], k, "expert") for k in range(1, 8)]


def slot_shards():
    return (lax.axis_index("dp") - jnp.arange(4)) % 4


def sum_turns(parts):
    own, above_by_three, two, above = parts
    far = turn(two, 1)
    back = turn(above_by_three, -1)
    near = turn((above.astype(F32) + far.astype(F32)).astype(BF), 1)
    return own.astype(F32) + near.astype(F32) + back.astype(F32)


def sum_shards(parts):
    return lax.psum_scatter(parts, "dp", scatter_dimension=0, tiled=False)


def sum_everywhere(array):
    if quick_expert() and quick_dp():
        array = array + swap(array, 1, "expert")
        for axis, scale in (("expert", 2), ("dp", 1)):
            one, two, three = (swap(array, scale * k, axis) for k in (1, 2, 3))
            array = (array + one) + (two + three)
        return array
    for axis in ("expert", "dp"):
        bits = 1
        while bits < lax.axis_size(axis):
            array = array + swap(array, bits, axis)
            bits *= 2
    return array


def cost(flops):
    return pl.CostEstimate(flops=flops, bytes_accessed=flops // 500, transcendentals=0)


def params():
    return pltpu.CompilerParams(
        dimension_semantics=("arbitrary",), vmem_limit_bytes=VMEM_BYTES
    )


def pair_scores(query, keys, key_place, query_place):
    scores = dot_nt(keys, query)
    return jnp.where(key_place <= query_place, scores, MASKED)


def attend_kernel(q_ref, k_ref, v_ref, kp_ref, qp_ref, mixed_ref, lse_ref):
    step = pl.program_id(0)
    keys, values = k_ref[...], v_ref[...]
    query = q_ref[...]
    lanes = lax.broadcasted_iota(jnp.int32, query.shape, 1)
    head_dim = query.shape[1] // 2
    scale = head_dim ** (-0.5)
    mixed = None
    for part in range(2):
        here = (lanes // head_dim) == part
        masked_query = jnp.where(here, query * scale, 0).astype(BF)
        scores = pair_scores(masked_query, keys, kp_ref[...], qp_ref[...])
        top = jnp.max(scores, axis=0, keepdims=True)
        weights = jnp.exp(scores - top)
        total = jnp.sum(weights, axis=0, keepdims=True)
        out = dot_tn(values, weights.astype(BF)) / total
        out = jnp.transpose(out)
        mixed = out if part == 0 else jnp.where(here, out, mixed)
        lse_ref[pl.ds(2 * step + part, 1), :] = top + jnp.log(total)
    mixed_ref[...] = mixed.astype(BF)


def attend(queries, keys, values, key_place, query_place):
    local, width = queries.shape
    group = keys.shape[0]
    pair = 2 * (width // HEADS)
    steps = HEADS // 2
    return pl.pallas_call(
        attend_kernel,
        grid=(steps,),
        in_specs=[
            pl.BlockSpec((local, pair), lambda i: (0, i)),
            pl.BlockSpec((group, pair), lambda i: (0, i)),
            pl.BlockSpec((group, pair), lambda i: (0, i)),
            pl.BlockSpec((group, 1), lambda i: (0, 0)),
            pl.BlockSpec((1, local), lambda i: (0, 0)),
        ],
        out_specs=[
            pl.BlockSpec((local, pair), lambda i: (0, i)),
            pl.BlockSpec((HEADS, local), lambda i: (0, 0)),
        ],
        out_shape=[
            jax.ShapeDtypeStruct((local, width), BF),
            jax.ShapeDtypeStruct((HEADS, local), F32),
        ],
        compiler_params=params(),
        cost_estimate=cost(1000),
        name="attend",
    )(queries, keys, values, key_place, query_place)


def attend_back_kernel(
    q_ref, k_ref, v_ref, do_ref, o_ref, lse_ref, kp_ref, qp_ref, dq_ref, dk_ref, dv_ref
):
    step = pl.program_id(0)
    keys, values = k_ref[...], v_ref[...]
    query, grad_out = q_ref[...], do_ref[...]
    lanes = lax.broadcasted_iota(jnp.int32, query.shape, 1)
    head_dim = query.shape[1] // 2
    scale = head_dim ** (-0.5)
    product = jnp.transpose(grad_out.astype(F32) * o_ref[...].astype(F32))
    grad_query = grad_keys = grad_values = None
    for part in range(2):
        here = (lanes // head_dim) == part
        masked_query = jnp.where(here, query * scale, 0).astype(BF)
        masked_grad = jnp.where(here, grad_out, 0).astype(BF)
        scores = pair_scores(masked_query, keys, kp_ref[...], qp_ref[...])
        weights = jnp.exp(scores - lse_ref[pl.ds(2 * step + part, 1), :])
        delta = jnp.sum(
            product[part * head_dim : (part + 1) * head_dim], axis=0, keepdims=True
        )
        grad_weights = dot_nt(values, masked_grad)
        grad_scores = (weights * (grad_weights - delta)).astype(BF)
        dq = jnp.transpose(dot_tn(keys, grad_scores)) * scale
        dk = dot_nn(grad_scores, masked_query)
        dv = dot_nn(weights.astype(BF), masked_grad)
        if part == 0:
            grad_query, grad_keys, grad_values = dq, dk, dv
        else:
            grad_query = jnp.where(here, dq, grad_query)
            grad_keys, grad_values = grad_keys + dk, grad_values + dv
    dq_ref[...] = grad_query.astype(BF)
    dk_ref[...] = grad_keys.astype(BF)
    dv_ref[...] = grad_values.astype(BF)


def attend_back(queries, keys, values, grad_out, mixed, lse, key_place, query_place):
    local, width = queries.shape
    group = keys.shape[0]
    pair = 2 * (width // HEADS)
    steps = HEADS // 2
    rows = pl.BlockSpec((local, pair), lambda i: (0, i))
    cols = pl.BlockSpec((group, pair), lambda i: (0, i))
    return pl.pallas_call(
        attend_back_kernel,
        grid=(steps,),
        in_specs=[
            rows,
            cols,
            cols,
            rows,
            rows,
            pl.BlockSpec((HEADS, local), lambda i: (0, 0)),
            pl.BlockSpec((group, 1), lambda i: (0, 0)),
            pl.BlockSpec((1, local), lambda i: (0, 0)),
        ],
        out_specs=[rows, cols, cols],
        out_shape=[
            jax.ShapeDtypeStruct((local, width), BF),
            jax.ShapeDtypeStruct((group, width), BF),
            jax.ShapeDtypeStruct((group, width), BF),
        ],
        compiler_params=params(),
        cost_estimate=cost(1000),
        name="attend_back",
    )(queries, keys, values, grad_out, mixed, lse, key_place, query_place)


def first_sum_kernel(
    six_ref, two_ref, four_ref, own_ref, six_o, two_o, four_o, own_o, six_a, six_b, two_a,
    four_b, two_f, four_f, mine
):
    half = six_a.shape[0]
    six = (six_ref[...].astype(F32) + six_o[...].astype(F32)).astype(BF)
    six_a[...], six_b[...] = six[:half], six[half:]
    two = two_ref[...].astype(F32) + two_o[...].astype(F32)
    two_a[...], two_f[...] = two[:half].astype(BF), two[half:]
    four = four_ref[...].astype(F32) + four_o[...].astype(F32)
    four_f[...], four_b[...] = four[:half], four[half:].astype(BF)
    mine[...] = own_ref[...].astype(F32) + own_o[...].astype(F32)


def place_kernel(spots, member_ref, *refs):
    pieces, out_ref = refs[: len(spots)], refs[len(spots)]
    half = out_ref.shape[2] // 2
    for i, (block, row) in enumerate(spots):
        owner = member_ref[0] ^ block
        columns = pl.ds(pl.multiple_of((owner % 2) * half, 128), half)
        out_ref[owner // 2, row : row + pieces[i].shape[0], columns] = pieces[i][...]


def place_halves(member, pieces):
    spots = [(block, row) for block, row, _ in pieces]
    arrays = [array for _, _, array in pieces]
    rows, half = arrays[0].shape
    return pl.pallas_call(
        functools.partial(place_kernel, spots),
        in_specs=[pl.BlockSpec(memory_space=pltpu.SMEM)]
        + [pl.BlockSpec(memory_space=pltpu.VMEM)] * len(arrays),
        out_specs=pl.BlockSpec(memory_space=pltpu.VMEM),
        out_shape=jax.ShapeDtypeStruct((4, rows, 2 * half), arrays[0].dtype),
        compiler_params=pltpu.CompilerParams(vmem_limit_bytes=VMEM_BYTES),
        cost_estimate=cost(1000),
        name="place_halves",
    )(member.reshape(1), *arrays)


def attn_weight_kernel(
    member_ref, x_ref, all_ref, mixed_ref, q_ref, k_ref, v_ref, branch_ref, out_ref
):
    owner = member_ref[0] ^ pl.program_id(0)
    half = out_ref.shape[2]
    columns = pl.ds(pl.multiple_of((owner % 2) * half, 128), half)
    sources = ((x_ref, q_ref), (all_ref, k_ref), (all_ref, v_ref), (mixed_ref, branch_ref))
    for kind, (left, right) in enumerate(sources):

        @pl.when(owner // 2 == kind)
        def _(left=left, right=right):
            out_ref[0] = dot_tn(left[...], right[:, columns]).astype(BF)


def attn_weight_back(member, *arrays):
    width = arrays[0].shape[1]
    return pl.pallas_call(
        attn_weight_kernel,
        grid=(8,),
        in_specs=[pl.BlockSpec(memory_space=pltpu.SMEM)]
        + [pl.BlockSpec(a.shape, lambda i: (0, 0)) for a in arrays],
        out_specs=pl.BlockSpec((1, width, width // 2), lambda i: (i, 0, 0)),
        out_shape=jax.ShapeDtypeStruct((8, width, width // 2), BF),
        compiler_params=params(),
        cost_estimate=cost(4 * (arrays[0].shape[0] + arrays[1].shape[0]) * width * width),
        name="attn_weight_back",
    )(member.reshape(1), *arrays)


def head_kernel(rows_ref, heads_ref, exps_ref, stats_ref):
    rows = rows_ref[...]
    count = heads_ref.shape[0]
    for k in range(count):
        scores = dot_nt(heads_ref[k], rows)
        top = jnp.max(scores, axis=0, keepdims=True)
        weights = jnp.exp(scores - top)
        stats_ref[k : k + 1, :] = top
        stats_ref[count + k : count + k + 1, :] = jnp.sum(weights, axis=0, keepdims=True)
        exps_ref[k] = weights.astype(BF)


def head_forward(rows, heads):
    group, width = rows.shape
    count, depth, _ = heads.shape
    block = min(512, group)
    exps, stats = pl.pallas_call(
        head_kernel,
        grid=(group // block,),
        in_specs=[
            pl.BlockSpec((block, width), lambda i: (i, 0)),
            pl.BlockSpec((count, depth, width), lambda i: (0, 0, 0)),
        ],
        out_specs=[
            pl.BlockSpec((count, depth, block), lambda i: (0, 0, i)),
            pl.BlockSpec((2 * count, block), lambda i: (0, i)),
        ],
        out_shape=[
            jax.ShapeDtypeStruct((count, depth, group), BF),
            jax.ShapeDtypeStruct((2 * count, group), F32),
        ],
        compiler_params=params(),
        cost_estimate=cost(2 * group * width * depth * count),
        name="head_forward",
    )(rows, heads)
    return exps, stats


def chosen_tokens(rank_ref, word_ref, k, turn_no, capacity):
    group = rank_ref.shape[1]
    place = lax.broadcasted_iota(jnp.int32, (capacity, group), 0) + turn_no * capacity
    chosen = rank_ref[k : k + 1, :] == place.astype(F32)
    word = jnp.sum(jnp.where(chosen, word_ref[...] + 1.0, 0.0), axis=1, keepdims=True) - 1.0
    return chosen, word


def word_hots(word, words):
    lanes = lax.broadcasted_iota(jnp.int32, (word.shape[0], words), 1).astype(F32)
    return (word == lanes).astype(BF)


def wanted_kernel(
    capacity, rounds_ref, rank_ref, word_ref, heads_ref, out_ref
):
    count, words, _ = heads_ref.shape

    def wanted(turn_no):
        picks, found = [], []
        for k in range(count):
            chosen, word = chosen_tokens(rank_ref, word_ref, k, turn_no, capacity)
            picks.append(jnp.where(chosen, 1.0, 0.0).astype(BF))
            found.append(dot_nn(word_hots(word, words), heads_ref[k]).astype(BF))
        return dot_tn(jnp.concatenate(picks), jnp.concatenate(found))

    out_ref[...] = wanted(0).astype(BF)

    @pl.loop(1, rounds_ref[0])
    def _(turn_no):
        out_ref[...] = (out_ref[...].astype(F32) + wanted(turn_no)).astype(BF)


def picked_kernel(rows_ref, wanted_ref, picked_ref):
    product = rows_ref[...].astype(F32) * wanted_ref[...].astype(F32)
    high = product.astype(BF)
    low = (product - high.astype(F32)).astype(BF)
    ones = jnp.ones((8, product.shape[1]), BF)
    picked = dot_nt(ones, high) + dot_nt(ones, low)
    picked_ref[...] = picked[0:1, :]


def stats_kernel(sums_ref, out_ref):
    count = sums_ref.shape[0] // 2
    tops = sums_ref[:count, :]
    top = jnp.max(tops, axis=0, keepdims=True)
    out_ref[0:1, :] = top
    out_ref[1:2, :] = jnp.sum(sums_ref[count:, :] * jnp.exp(tops - top), axis=0, keepdims=True)


def scale_kernel(orders, sums_ref, weight_ref, *refs):
    count = sums_ref.shape[0] // 2
    stats, logsum_ref, columns_ref = refs[: len(orders)], refs[-2], refs[-1]
    length = sums_ref.shape[1] // len(orders)
    tops, sums = [], []
    for ref, order in zip(stats, orders):
        pieces = [ref[:, j * length : (j + 1) * length] for j in order]
        together = jnp.concatenate(pieces, axis=1)
        tops.append(together[0:1, :])
        sums.append(together[1:2, :])
    top = functools.reduce(jnp.maximum, tops)
    total = sum(s * jnp.exp(t - top) for s, t in zip(sums, tops))
    logsum = top + jnp.log(total)
    logsum_ref[...] = logsum
    weight = weight_ref[...]
    scales = weight * jnp.exp(sums_ref[:count, :] - logsum)
    rest = columns_ref.shape[1] - count - 1
    columns_ref[...] = jnp.transpose(
        jnp.concatenate([scales, weight, jnp.zeros((rest, weight.shape[1]), F32)], axis=0)
    )


def head_weight_kernel(exps_ref, rows_ref, columns_ref, terms_ref, out_ref):
    lanes = lax.broadcasted_iota(jnp.int32, columns_ref.shape, 1)
    mine = jnp.where(lanes == pl.program_id(0), columns_ref[...], 0.0)
    scaled = (rows_ref[...].astype(F32) * jnp.sum(mine, axis=1, keepdims=True)).astype(BF)
    out_ref[0] = (dot_nn(exps_ref[0], scaled) - terms_ref[0].astype(F32)).astype(BF)


def head_weight_back(exps, rows, columns, terms):
    count, depth, group = exps.shape
    width = rows.shape[1]
    return pl.pallas_call(
        head_weight_kernel,
        grid=(count,),
        in_specs=[
            pl.BlockSpec((1, depth, group), lambda i: (i, 0, 0)),
            pl.BlockSpec((group, width), lambda i: (0, 0)),
            pl.BlockSpec(columns.shape, lambda i: (0, 0)),
            pl.BlockSpec((1, depth, width), lambda i: (i, 0, 0)),
        ],
        out_specs=pl.BlockSpec((1, depth, width), lambda i: (i, 0, 0)),
        out_shape=jax.ShapeDtypeStruct((count, depth, width), BF),
        compiler_params=params(),
        cost_estimate=cost(2 * group * width * depth * count),
        name="head_weight_back",
    )(exps, rows, columns, terms)


def target_kernel(capacity, rounds_ref, rank_ref, word_ref, weight_ref, rows_ref, out_ref):
    count, words, _ = out_ref.shape

    def term(k, turn_no):
        chosen, word = chosen_tokens(rank_ref, word_ref, k, turn_no, capacity)
        weight = jnp.sum(jnp.where(chosen, weight_ref[...], 0.0), axis=1, keepdims=True)
        found = dot_nn(jnp.where(chosen, 1.0, 0.0).astype(BF), rows_ref[...]) * weight
        return dot_tn(word_hots(word, words), found.astype(BF))

    for k in range(count):
        out_ref[k] = term(k, 0).astype(BF)

    @pl.loop(1, rounds_ref[0])
    def _(turn_no):
        for k in range(count):
            out_ref[k] = (out_ref[k].astype(F32) + term(k, turn_no)).astype(BF)


def whole_call(kernel, out_shape, name, *arrays):
    vmem = pl.BlockSpec(memory_space=pltpu.VMEM)
    smem = pl.BlockSpec(memory_space=pltpu.SMEM)
    return pl.pallas_call(
        kernel,
        in_specs=[smem if a.dtype == jnp.int32 else vmem for a in arrays],
        out_specs=jax.tree.map(lambda _: vmem, out_shape),
        out_shape=out_shape,
        compiler_params=pltpu.CompilerParams(vmem_limit_bytes=VMEM_BYTES),
        cost_estimate=cost(1000),
        name=name,
    )(*arrays)


def head_rows_kernel(columns_ref, wanted_ref, heads_ref, exps_ref, out_ref):
    count = heads_ref.shape[0]
    out = wanted_ref[...].astype(F32) * (-columns_ref[:, count : count + 1])
    for k in range(count):
        out = out + dot_tn(exps_ref[k], heads_ref[k]) * columns_ref[:, k : k + 1]
    out_ref[...] = out.astype(BF)


def head_rows_back(columns, wanted, heads, exps):
    count, depth, width = heads.shape
    group = exps.shape[2]
    block = min(256, group)
    rows = pl.BlockSpec((block, width), lambda i: (i, 0))
    return pl.pallas_call(
        head_rows_kernel,
        grid=(group // block,),
        in_specs=[
            pl.BlockSpec((block, columns.shape[1]), lambda i: (i, 0)),
            rows,
            pl.BlockSpec((count, depth, width), lambda i: (0, 0, 0)),
            pl.BlockSpec((count, depth, block), lambda i: (0, 0, i)),
        ],
        out_specs=rows,
        out_shape=jax.ShapeDtypeStruct((group, width), BF),
        compiler_params=params(),
        cost_estimate=cost(2 * group * width * depth * count),
        name="head_rows_back",
    )(columns, wanted, heads, exps)


def ranks(hits):
    count, length = hits.shape
    cut = hits.reshape(count, length // 128, 128)
    ones = cut.astype(BF)
    before = (jnp.arange(128)[:, None] < jnp.arange(128)[None, :]).astype(BF)
    inner = lax.dot_general(ones, before, (((2,), (0,)), ((), ())), preferred_element_type=F32)
    sums = jnp.sum(ones.astype(F32), axis=2)
    earlier = jnp.arange(length // 128)[:, None] > jnp.arange(length // 128)[None, :]
    outer = jnp.sum(jnp.where(earlier[None], sums[:, None, :], 0.0), axis=2)
    return jnp.where(cut, inner + outer[..., None], -1.0).reshape(count, length)


def split_high_low(values):
    high = lax.reduce_precision(values, 8, 7)
    return high.astype(BF), (values - high).astype(BF)


def body(
    ids,
    targets,
    loss_mask,
    domain_ids,
    expert_lists,
    tables,
    tables_m,
    tables_v,
    attn,
    attn_m,
    attn_v,
    experts,
    experts_m,
    experts_v,
    router,
    router_m,
    router_v,
    gains,
    gains_m,
    gains_v,
):
    shards = lax.axis_size("expert")
    rows_dp = lax.axis_size("dp")
    member = lax.axis_index("expert")
    batch_row = lax.axis_index("dp")
    group = ids.shape[0]
    local = group // shards
    own = member * local
    width = gains.shape[1]
    slots = expert_lists.shape[3]
    words = tables.shape[1]
    order = block_order()

    attn_b = attn.astype(BF)
    if quick_expert() and quick_dp():
        mine = lax.dynamic_slice(
            attn_b,
            (member // 2, 0, (member % 2) * (width // 2)),
            (1, attn.shape[1], width // 2),
        )[0]
        below, above = turn(mine, 1), turn(mine, -1)
        attn_parts = jnp.stack([mine, below, turn(below, 1), above])
        attn_parts = attn_parts[slot_shards()].reshape(width, width // 2)
        attn_pieces = gather_pieces(attn_parts)
    table_b = tables[0].astype(BF)
    experts_b = experts[0].astype(BF)
    head_b = tables[1].astype(BF)

    capacity = min(group, 3 * group // (2 * shards * rows_dp))
    capacity = -(-capacity // 16) * 16
    ids_dp = jnp.stack([ids] + [turn(ids, k) for k in range(1, rows_dp)])
    first_word = (member * rows_dp + batch_row) * words
    ids_own = ids_dp - first_word
    rank_own = ranks((ids_own >= 0) & (ids_own < words))
    ids_own = ids_own.astype(F32)
    place = jnp.arange(capacity, dtype=F32)
    owners = (batch_row + jnp.arange(rows_dp)) % rows_dp
    ids_from = ids[None, :] - ((member * rows_dp + owners) * words)[:, None]
    rank_from = ranks((ids_from >= 0) & (ids_from < words))
    rank_from = rank_from.reshape(rows_dp, shards, local)[:, order].reshape(rows_dp, group)
    owner_of = ids_dp // words
    owner_hits = owner_of[:, None, :] == jnp.arange(shards * rows_dp)[None, :, None]
    most = jnp.max(jnp.sum(owner_hits.astype(F32), axis=2)).astype(jnp.int32)
    rounds = (most + capacity - 1) // capacity

    def own_select(turn_no):
        chosen = rank_own[:, None, :] == (place + turn_no * capacity)[None, :, None]
        at = jnp.sum(jnp.where(chosen, ids_own[:, None, :] + 1.0, 0.0), axis=2) - 1.0
        at = at.reshape(-1)[:, None]
        return (at == jnp.arange(words, dtype=F32)[None, :]).astype(BF)

    def from_select(turn_no):
        chosen = rank_from[:, None, :] == (place + turn_no * capacity)[None, :, None]
        return chosen.reshape(-1, group).astype(BF)

    def look_up(select_own):
        found = dot_nn(select_own, table_b).astype(BF).reshape(rows_dp, capacity, width)
        arrived = [found[0]] + [turn(found[k], -k) for k in range(1, rows_dp)]
        return jnp.concatenate(arrived)

    def put(arrived, select_from):
        return dot_tn(select_from, arrived).astype(BF)

    def spread(turn_no, grads, select_own, select_from):
        chosen = dot_nn(select_from, grads).astype(BF).reshape(rows_dp, capacity, width)
        arrived = [chosen[0]] + [turn(chosen[k], k) for k in range(1, rows_dp)]
        return dot_tn(select_own, jnp.concatenate(arrived))

    targets_mine = targets.reshape(shards, local)[order].reshape(-1)
    word = targets_mine - member * (rows_dp * words)
    word_slot = jnp.where((word >= 0) & (word < rows_dp * words), word // words, rows_dp)
    word_row = (word % words).astype(F32)[None, :]
    word_hits = word_slot[None, :] == jnp.arange(rows_dp)[:, None]
    word_rank = ranks(word_hits)
    word_most = jnp.max(jnp.sum(word_hits.astype(F32), axis=1)).astype(jnp.int32)
    word_rounds = ((word_most + capacity - 1) // capacity).reshape(1)

    def token_weights():
        everything = loss_mask.shape[0]
        domain_of = jnp.take(domain_ids, jnp.arange(everything) // SEQ)
        hits = ((domain_of[:, None] == jnp.arange(NDOM)[None, :]) & (loss_mask[:, None] > 0)).astype(
            F32
        )
        counts = jnp.sum(hits, axis=0)
        domain_weight = 10.0 * (NDOM - jnp.arange(NDOM)).astype(F32) / jnp.maximum(counts, 1.0)
        group_hits = lax.dynamic_slice_in_dim(hits, batch_row * group, group, 0)
        group_hits = group_hits.reshape(shards, local, NDOM)[order].reshape(group, NDOM)
        token_weight = jnp.sum(group_hits * domain_weight[None, :], axis=1)
        return token_weight, group_hits, counts

    token_weight, group_hits, counts = token_weights()
    lists = expert_lists[0, 0][order]
    hot = lists[:, :, None] == jnp.arange(local)[None, None, :]
    hot_b = hot.reshape(-1, local).astype(BF)
    select_own = own_select(0)
    select_from = from_select(0)
    quick = quick_expert() and quick_dp()
    arrived = look_up(select_own)
    expert_shards = lax.all_gather(experts_b, "dp")
    looked = put(arrived, select_from)
    _, looked = lax.while_loop(
        lambda state: state[0] < rounds,
        lambda state: (
            state[0] + 1,
            state[1]
            + put(
                look_up(own_select(state[0].astype(F32))),
                from_select(state[0].astype(F32)),
            ),
        ),
        (jnp.int32(1), looked),
    )
    if quick_expert() and quick_dp():
        attn_full = place_halves(member, attn_pieces)
    else:
        attn_full = lax.all_gather(attn_b, "dp", axis=1, tiled=True)
    embedded = sum_blocks(split_blocks(looked))
    router_b = router.astype(BF)

    normed_ab = normed(embedded, gains[0]).astype(BF)
    normed_all = gather_rows(normed_ab)
    queries = dot_nn(normed_ab, attn_full[0]).astype(BF)
    keys = dot_nn(normed_all, attn_full[1]).astype(BF)
    values = dot_nn(normed_all, attn_full[2]).astype(BF)
    token_place = (order[:, None] * local + jnp.arange(local)[None, :]).reshape(-1)
    seq_start = own // SEQ * SEQ
    key_place = jnp.where(token_place >= seq_start, token_place, group)[:, None]
    query_place = (own + jnp.arange(local))[None, :]
    mixed_b, logsum = attend(queries, keys, values, key_place, query_place)
    resid_one = embedded + dot_nn(mixed_b, attn_full[3])

    normed_bb = normed(resid_one, gains[1]).astype(BF)
    router_logits = dot_nn(normed_bb, router_b)
    gates = jax.nn.softmax(router_logits, axis=-1)
    gates_mine = jnp.transpose(gates[:, order])
    gate_table = jnp.where(hot, gates_mine[:, None, :], 0.0)
    slot_gates = jnp.sum(gate_table, axis=2).reshape(-1, 1)
    gate_high, gate_low = split_high_low(gate_table.reshape(-1, local))
    send = dot_nn(hot_b, normed_bb).astype(BF)
    received = exchange(split_blocks(send))
    head_shards = lax.all_gather(after(head_b, (expert_shards, received[1])), "dp")
    received = jnp.concatenate(received)
    pres, hiddens, produced = [], [], None
    for shard in expert_shards:
        pre = dot_nn(received, shard[0])
        hidden = gelu(pre).astype(BF)
        term = dot_nt(hidden, shard[1])
        produced = term if produced is None else produced + term
        pres.append(pre)
        hiddens.append(hidden)
    returned = jnp.concatenate(exchange(split_blocks(produced.astype(BF))))
    mixture = dot_tn(gate_high, returned) + dot_tn(gate_low, returned)
    resid_two = resid_one + mixture
    normed_cb = normed(resid_two, gains[2]).astype(BF)

    rows_all = gather_rows(normed_cb)
    target_terms = whole_call(
        functools.partial(target_kernel, capacity),
        jax.ShapeDtypeStruct((rows_dp, words, width), BF),
        "target_terms",
        word_rounds,
        word_rank,
        word_row,
        token_weight[None, :],
        rows_all,
    )
    exps, head_stats = head_forward(after(rows_all, target_terms), head_shards)
    stats = whole_call(
        stats_kernel, jax.ShapeDtypeStruct((2, group), F32), "head_stats", head_stats
    )
    if quick_expert():
        gathered = [stats] + [swap(stats, k, "expert") for k in range(1, 8)]
        orders = [[j ^ k for j in range(8)] for k in range(8)]
    else:
        gathered = list(lax.all_gather(stats, "expert"))
        orders = [list(range(shards))] * shards
    wanted = whole_call(
        functools.partial(wanted_kernel, capacity),
        jax.ShapeDtypeStruct((group, width), BF),
        "wanted_rows",
        word_rounds,
        word_rank,
        word_row,
        head_shards,
    )
    logsum_tok, columns = whole_call(
        functools.partial(scale_kernel, orders),
        (
            jax.ShapeDtypeStruct((1, group), F32),
            jax.ShapeDtypeStruct((group, -(-(rows_dp + 1) // 8) * 8), F32),
        ),
        "head_scales",
        head_stats,
        token_weight[None, :],
        *gathered,
    )
    own_block = 0 if quick_expert() else member
    grad_rows_c = head_rows_back(columns, wanted, head_shards, exps)
    grad_heads = head_weight_back(exps, rows_all, columns, target_terms)
    grad_head = sum_shards(grad_heads)
    picked = whole_call(
        picked_kernel,
        jax.ShapeDtypeStruct((1, group), F32),
        "picked_logits",
        after(rows_all, grad_heads),
        wanted,
    )
    own_sums = jnp.sum(
        lax.dynamic_slice_in_dim(group_hits, own_block * local, local, 0)
        * lax.dynamic_slice_in_dim(logsum_tok[0], own_block * local, local, 0)[:, None],
        axis=0,
    ) - jnp.sum(group_hits * picked[0][:, None], axis=0)
    grad_normed_c = sum_blocks(split_blocks(grad_rows_c))
    grad_two, grad_gain_c = norm_back(resid_two, gains[2], grad_normed_c)

    two_high, two_low = split_high_low(grad_two)
    grad_slot = dot_nn(hot_b, two_high) + dot_nn(hot_b, two_low)
    grad_gate_slot = jnp.sum(grad_slot * returned.astype(F32), axis=-1)
    grad_produced = jnp.concatenate(
        exchange(split_blocks((grad_slot * slot_gates).astype(BF)))
    )
    grad_pres, grad_sent = [], None
    for k in range(rows_dp):
        grad_hidden = dot_nn(grad_produced, expert_shards[k, 1])
        _, gelu_pull = jax.vjp(gelu, pres[k])
        grad_pres.append(gelu_pull(grad_hidden)[0].astype(BF))
        term = dot_nt(grad_pres[k], expert_shards[k, 0])
        grad_sent = term if grad_sent is None else grad_sent + term
    grad_sent = grad_sent.astype(BF)
    late_produced, late_received = after((grad_produced, received), grad_sent)
    grad_parts = []
    for grad_pre, hidden in zip(grad_pres, hiddens):
        grad_parts.append(dot_tn(late_received, grad_pre).astype(BF))
        grad_parts.append(dot_tn(late_produced, hidden).astype(BF))
    grad_parts = jnp.stack(grad_parts).reshape(rows_dp, 2, width, -1)
    grad_experts = sum_shards(grad_parts)[None]
    grad_back = jnp.concatenate(exchange(split_blocks(grad_sent)))
    grad_normed_b = dot_tn(hot_b, grad_back)
    grad_gates = jnp.sum(
        jnp.where(hot, grad_gate_slot.reshape(shards, slots)[:, :, None], 0.0), axis=1
    )
    grad_gates = jnp.transpose(grad_gates[order])
    _, soft_pull = jax.vjp(lambda logit_rows: jax.nn.softmax(logit_rows, axis=-1), router_logits)
    grad_router_logits = soft_pull(grad_gates)[0].astype(BF)
    grad_router = dot_tn(normed_bb, grad_router_logits)
    grad_normed_b = grad_normed_b + dot_nt(grad_router_logits, router_b)
    normal_back, grad_gain_b = norm_back(resid_one, gains[1], grad_normed_b)
    grad_one = grad_two + normal_back

    grad_branch = grad_one.astype(BF)
    grad_mixed = dot_nt(grad_branch, attn_full[3]).astype(BF)
    grad_query, grad_keys, grad_values = attend_back(
        queries, keys, values, grad_mixed, mixed_b, logsum, key_place, query_place
    )
    grad_normed_rows = dot_nt(grad_keys, attn_full[1]) + dot_nt(grad_values, attn_full[2])
    firsts = []
    grad_normed_a = sum_blocks(split_blocks(grad_normed_rows.astype(BF)), firsts)
    grad_normed_a = grad_normed_a + dot_nt(grad_query, attn_full[0])
    normal_front, grad_gain_a = norm_back(embedded, gains[0], grad_normed_a)
    grad_embedded = (grad_one + normal_front).astype(BF)
    grad_embedded_all = gather_rows(grad_embedded)
    grad_embed = spread(0, grad_embedded_all, select_own, select_from)
    _, grad_embed = lax.while_loop(
        lambda state: state[0] < rounds,
        lambda state: (
            state[0] + 1,
            state[1]
            + spread(
                state[0],
                grad_embedded_all,
                own_select(state[0].astype(F32)),
                from_select(state[0].astype(F32)),
            ),
        ),
        (jnp.int32(1), grad_embed),
    )
    if quick_expert() and quick_dp():
        blocks = attn_weight_back(
            member,
            normed_ab,
            after(normed_all, firsts[0]),
            mixed_b,
            grad_query,
            grad_keys,
            grad_values,
            grad_branch,
        )
        blocks = after(blocks, grad_embedded_all)
        part = sum_blocks([blocks[j] for j in range(8)]).astype(BF)
        part = part.reshape(4, width // 4, width // 2)[slot_shards()]
        part = sum_turns([part[k] for k in range(4)])
        attn_squares = jnp.sum(part * part)
        grad_attn = place_halves(member, gather_pieces(part.astype(BF)))
    else:
        grad_attn = jnp.stack(
            [
                dot_tn(normed_ab, grad_query),
                dot_tn(normed_all, grad_keys),
                dot_tn(normed_all, grad_values),
                dot_tn(mixed_b, grad_branch),
            ]
        ).astype(BF)
        grad_attn = lax.psum_scatter(grad_attn, "dp", scatter_dimension=1, tiled=True)
        grad_attn = lax.psum(grad_attn, "expert")
        attn_squares = jnp.sum(jnp.square(grad_attn.astype(F32))) / shards
    small = jnp.concatenate(
        [grad_router.reshape(-1), grad_gain_a, grad_gain_b, grad_gain_c, own_sums]
    )
    small = after(small, grad_embedded_all)
    small = jnp.pad(small, (0, -small.shape[0] % 1024)).reshape(-1, 128)
    small = sum_everywhere(small).reshape(-1)
    edge = router.size
    grad_router = small[:edge].reshape(router.shape)
    grad_gains = small[edge : edge + 3 * width].reshape(3, width)
    domain_sums = small[edge + 3 * width : edge + 3 * width + NDOM]
    small_squares = jnp.sum(grad_router * grad_router) + jnp.sum(grad_gains * grad_gains)
    grad_head = grad_head.astype(F32)
    head_squares = jnp.sum(grad_head * grad_head)
    grad_experts = after(grad_experts, (small, small_squares, grad_head, head_squares))
    grad_experts = grad_experts.astype(F32)
    squares = (
        jnp.sum(grad_embed * grad_embed)
        + head_squares
        + jnp.sum(grad_experts * grad_experts)
        + attn_squares
    )
    squares = sum_everywhere(jnp.broadcast_to(squares, (1, 128)))[0, 0]
    grad_norm = jnp.sqrt(squares + small_squares)
    factor = jnp.minimum(1.0, CLIP / (grad_norm + 1e-06))
    grad_tables = jnp.stack([grad_embed, grad_head])
    tables_out = adam(tables, grad_tables * factor, tables_m, tables_v, 0.1, 0.01)
    attn_out = adam(attn, grad_attn.astype(F32) * factor, attn_m, attn_v, 0.1, 0.01)
    experts_out = adam(experts, grad_experts * factor, experts_m, experts_v, 0.1, 0.01)
    router_out = adam(router, grad_router * factor, router_m, router_v, 0.04, 0.01)
    gains_out = adam(gains, grad_gains * factor, gains_m, gains_v, 0.4, 0.0)
    return (
        domain_sums,
        counts,
        grad_norm,
        *tables_out,
        *attn_out,
        *experts_out,
        *router_out,
        *gains_out,
    )


def solution(mesh):
    table = P(None, ("expert", "dp"), None)
    attn = P(None, "dp", None)
    expert = P("expert", None, None, "dp")
    in_specs = (
        P("dp"),
        P("dp"),
        P(),
        P(),
        P("dp", "expert", None, None),
        *[table] * 3,
        *[attn] * 3,
        *[expert] * 3,
        *[P()] * 6,
    )
    out_specs = (*[P()] * 3, *[table] * 4, *[attn] * 4, *[expert] * 4, *[P()] * 8)
    return jax.shard_map(body, mesh=mesh, in_specs=in_specs, out_specs=out_specs, check_vma=False)
```

```python
import functools

import jax
import jax.numpy as jnp
from jax import lax
from jax.experimental import pallas as pl
from jax.experimental.pallas import tpu as pltpu
from jax.sharding import PartitionSpec as P

HEADS = 12
SEQ = 2048
NDOM = 4
STEP = 10


NORM_EPS = 1e-05
BETA = 0.5
ADAM_EPS = 1e-08
CLIP = 1.0
MASKED = -1e30
BF = jnp.bfloat16
F32 = jnp.float32
VMEM_BYTES = 56 * 1024 * 1024


def normed(values, gain):
    return values * lax.rsqrt(jnp.mean(values * values, axis=-1, keepdims=True) + NORM_EPS) * gain


def norm_back(values, gain, grad):
    _, pull = jax.vjp(normed, values, gain)
    return pull(grad)


def gelu(values):
    return jax.nn.gelu(values, approximate=True)


def adam(weight, grad, first, second, rate, decay):
    first = BETA * first + (1.0 - BETA) * grad
    second = BETA * second + (1.0 - BETA) * grad * grad
    correct = 1.0 - BETA**STEP
    weight = weight - rate * (
        first / correct / (jnp.sqrt(second / correct) + ADAM_EPS) + decay * weight
    )
    return (first, second, weight, weight.astype(BF))


def dot(a, b, contract):
    return lax.dot_general(a, b, ((contract[0], contract[1]), ((), ())), preferred_element_type=F32)


def dot_nn(a, b):
    return dot(a, b, ((1,), (0,)))


def dot_nt(a, b):
    return dot(a, b, ((1,), (1,)))


def dot_tn(a, b):
    return dot(a, b, ((0,), (0,)))


def after(array, earlier):
    return array if earlier is None else lax.optimization_barrier((array, earlier))[0]


def swap(array, bits, axis):
    pairs = [(i, i ^ bits) for i in range(lax.axis_size(axis))]
    return lax.ppermute(array, axis, pairs)


def turn(array, steps):
    count = lax.axis_size("dp")
    return lax.ppermute(array, "dp", [(i, (i + steps) % count) for i in range(count)])


def quick_expert():
    return lax.axis_size("expert") == 8


def quick_dp():
    return lax.axis_size("dp") == 4


def block_order():
    count = lax.axis_size("expert")
    if quick_expert():
        return lax.axis_index("expert") ^ jnp.arange(count)
    return jnp.arange(count)


def gather_pieces(rows):
    count = lax.axis_size("expert")
    if not quick_expert():
        gathered = lax.all_gather(rows, "expert")
        return [(i, 0, gathered[i]) for i in range(count)]
    half = rows.shape[0] // 2
    one, two, four = (swap(rows, bits, "expert") for bits in (1, 2, 4))
    six_a = swap(two[:half], 4, "expert")
    six_b = swap(four[half:], 2, "expert")
    three = swap(two, 1, "expert")
    five = swap(four, 1, "expert")
    seven_a = swap(six_a, 1, "expert")
    seven_b = swap(six_b, 1, "expert")
    return [
        (0, 0, rows),
        (1, 0, one),
        (2, 0, two),
        (3, 0, three),
        (4, 0, four),
        (5, 0, five),
        (6, 0, six_a),
        (6, half, six_b),
        (7, 0, seven_a),
        (7, half, seven_b),
    ]


def gather_rows(rows):
    return jnp.concatenate([piece for _, _, piece in gather_pieces(rows)])


def sum_blocks(blocks, firsts=None):
    if not quick_expert():
        return lax.psum_scatter(
            jnp.stack(blocks), "expert", scatter_dimension=0, tiled=False
        ).astype(F32)
    half = blocks[0].shape[0] // 2
    width = blocks[0].shape[1]
    other = [swap(blocks[j], 1, "expert") for j in (7, 3, 5, 1)]
    piece, piece_f = (jax.ShapeDtypeStruct((half, width), t) for t in (BF, F32))
    six_a, six_b, two_a, four_b, two_f, four_f, mine = whole_call(
        first_sum_kernel,
        [piece] * 4 + [piece_f] * 2 + [jax.ShapeDtypeStruct((2 * half, width), F32)],
        "first_sum",
        *[blocks[j] for j in (6, 2, 4, 0)],
        *other,
    )
    if firsts is not None:
        firsts.append((six_a, two_a))
    six_a = swap(six_a, 2, "expert")
    six_b = swap(six_b, 4, "expert")
    two_a = swap(two_a, 2, "expert")
    four_b = swap(four_b, 4, "expert")
    four_a = swap((four_f + six_a.astype(F32)).astype(BF), 4, "expert")
    two_b = swap((two_f + six_b.astype(F32)).astype(BF), 2, "expert")
    return mine + jnp.concatenate(
        [
            two_a.astype(F32) + four_a.astype(F32),
            two_b.astype(F32) + four_b.astype(F32),
        ]
    )


def split_blocks(rows):
    count = lax.axis_size("expert")
    size = rows.shape[0] // count
    return [rows[i * size : (i + 1) * size] for i in range(count)]


def exchange(blocks):
    if not quick_expert():
        swapped = lax.all_to_all(jnp.stack(blocks), "expert", split_axis=0, concat_axis=0)
        return [swapped[i] for i in range(len(blocks))]
    return [blocks[0]] + [swap(blocks[k], k, "expert") for k in range(1, 8)]


def slot_shards():
    return (lax.axis_index("dp") - jnp.arange(4)) % 4


def sum_turns(parts):
    own, above_by_three, two, above = parts
    far = turn(two, 1)
    back = turn(above_by_three, -1)
    near = turn((above.astype(F32) + far.astype(F32)).astype(BF), 1)
    return own.astype(F32) + near.astype(F32) + back.astype(F32)


def sum_shards(parts):
    return lax.psum_scatter(parts, "dp", scatter_dimension=0, tiled=False)


def sum_everywhere(array):
    if quick_expert() and quick_dp():
        array = array + swap(array, 1, "expert")
        for axis, scale in (("expert", 2), ("dp", 1)):
            one, two, three = (swap(array, scale * k, axis) for k in (1, 2, 3))
            array = (array + one) + (two + three)
        return array
    for axis in ("expert", "dp"):
        bits = 1
        while bits < lax.axis_size(axis):
            array = array + swap(array, bits, axis)
            bits *= 2
    return array


def cost(flops):
    return pl.CostEstimate(flops=flops, bytes_accessed=flops // 500, transcendentals=0)


def params():
    return pltpu.CompilerParams(
        dimension_semantics=("arbitrary",), vmem_limit_bytes=VMEM_BYTES
    )


def pair_scores(query, keys, key_place, query_place):
    scores = dot_nt(keys, query)
    return jnp.where(key_place <= query_place, scores, MASKED)


def attend_kernel(q_ref, k_ref, v_ref, kp_ref, qp_ref, mixed_ref, lse_ref):
    step = pl.program_id(0)
    keys, values = k_ref[...], v_ref[...]
    query = q_ref[...]
    lanes = lax.broadcasted_iota(jnp.int32, query.shape, 1)
    head_dim = query.shape[1] // 2
    scale = head_dim ** (-0.5)
    mixed = None
    for part in range(2):
        here = (lanes // head_dim) == part
        masked_query = jnp.where(here, query * scale, 0).astype(BF)
        scores = pair_scores(masked_query, keys, kp_ref[...], qp_ref[...])
        top = jnp.max(scores, axis=0, keepdims=True)
        weights = jnp.exp(scores - top)
        total = jnp.sum(weights, axis=0, keepdims=True)
        out = dot_tn(values, weights.astype(BF)) / total
        out = jnp.transpose(out)
        mixed = out if part == 0 else jnp.where(here, out, mixed)
        lse_ref[pl.ds(2 * step + part, 1), :] = top + jnp.log(total)
    mixed_ref[...] = mixed.astype(BF)


def attend(queries, keys, values, key_place, query_place):
    local, width = queries.shape
    group = keys.shape[0]
    pair = 2 * (width // HEADS)
    steps = HEADS // 2
    return pl.pallas_call(
        attend_kernel,
        grid=(steps,),
        in_specs=[
            pl.BlockSpec((local, pair), lambda i: (0, i)),
            pl.BlockSpec((group, pair), lambda i: (0, i)),
            pl.BlockSpec((group, pair), lambda i: (0, i)),
            pl.BlockSpec((group, 1), lambda i: (0, 0)),
            pl.BlockSpec((1, local), lambda i: (0, 0)),
        ],
        out_specs=[
            pl.BlockSpec((local, pair), lambda i: (0, i)),
            pl.BlockSpec((HEADS, local), lambda i: (0, 0)),
        ],
        out_shape=[
            jax.ShapeDtypeStruct((local, width), BF),
            jax.ShapeDtypeStruct((HEADS, local), F32),
        ],
        compiler_params=params(),
        cost_estimate=cost(1000),
        name="attend",
    )(queries, keys, values, key_place, query_place)


def attend_back_kernel(
    q_ref, k_ref, v_ref, do_ref, o_ref, lse_ref, kp_ref, qp_ref, dq_ref, dk_ref, dv_ref
):
    step = pl.program_id(0)
    keys, values = k_ref[...], v_ref[...]
    query, grad_out = q_ref[...], do_ref[...]
    lanes = lax.broadcasted_iota(jnp.int32, query.shape, 1)
    head_dim = query.shape[1] // 2
    scale = head_dim ** (-0.5)
    product = jnp.transpose(grad_out.astype(F32) * o_ref[...].astype(F32))
    grad_query = grad_keys = grad_values = None
    for part in range(2):
        here = (lanes // head_dim) == part
        masked_query = jnp.where(here, query * scale, 0).astype(BF)
        masked_grad = jnp.where(here, grad_out, 0).astype(BF)
        scores = pair_scores(masked_query, keys, kp_ref[...], qp_ref[...])
        weights = jnp.exp(scores - lse_ref[pl.ds(2 * step + part, 1), :])
        delta = jnp.sum(
            product[part * head_dim : (part + 1) * head_dim], axis=0, keepdims=True
        )
        grad_weights = dot_nt(values, masked_grad)
        grad_scores = (weights * (grad_weights - delta)).astype(BF)
        dq = jnp.transpose(dot_tn(keys, grad_scores)) * scale
        dk = dot_nn(grad_scores, masked_query)
        dv = dot_nn(weights.astype(BF), masked_grad)
        if part == 0:
            grad_query, grad_keys, grad_values = dq, dk, dv
        else:
            grad_query = jnp.where(here, dq, grad_query)
            grad_keys, grad_values = grad_keys + dk, grad_values + dv
    dq_ref[...] = grad_query.astype(BF)
    dk_ref[...] = grad_keys.astype(BF)
    dv_ref[...] = grad_values.astype(BF)


def attend_back(queries, keys, values, grad_out, mixed, lse, key_place, query_place):
    local, width = queries.shape
    group = keys.shape[0]
    pair = 2 * (width // HEADS)
    steps = HEADS // 2
    rows = pl.BlockSpec((local, pair), lambda i: (0, i))
    cols = pl.BlockSpec((group, pair), lambda i: (0, i))
    return pl.pallas_call(
        attend_back_kernel,
        grid=(steps,),
        in_specs=[
            rows,
            cols,
            cols,
            rows,
            rows,
            pl.BlockSpec((HEADS, local), lambda i: (0, 0)),
            pl.BlockSpec((group, 1), lambda i: (0, 0)),
            pl.BlockSpec((1, local), lambda i: (0, 0)),
        ],
        out_specs=[rows, cols, cols],
        out_shape=[
            jax.ShapeDtypeStruct((local, width), BF),
            jax.ShapeDtypeStruct((group, width), BF),
            jax.ShapeDtypeStruct((group, width), BF),
        ],
        compiler_params=params(),
        cost_estimate=cost(1000),
        name="attend_back",
    )(queries, keys, values, grad_out, mixed, lse, key_place, query_place)


def first_sum_kernel(
    six_ref, two_ref, four_ref, own_ref, six_o, two_o, four_o, own_o, six_a, six_b, two_a,
    four_b, two_f, four_f, mine
):
    half = six_a.shape[0]
    six = (six_ref[...].astype(F32) + six_o[...].astype(F32)).astype(BF)
    six_a[...], six_b[...] = six[:half], six[half:]
    two = two_ref[...].astype(F32) + two_o[...].astype(F32)
    two_a[...], two_f[...] = two[:half].astype(BF), two[half:]
    four = four_ref[...].astype(F32) + four_o[...].astype(F32)
    four_f[...], four_b[...] = four[:half], four[half:].astype(BF)
    mine[...] = own_ref[...].astype(F32) + own_o[...].astype(F32)


def place_kernel(spots, member_ref, *refs):
    pieces, out_ref = refs[: len(spots)], refs[len(spots)]
    half = out_ref.shape[2] // 2
    for i, (block, row) in enumerate(spots):
        owner = member_ref[0] ^ block
        columns = pl.ds(pl.multiple_of((owner % 2) * half, 128), half)
        out_ref[owner // 2, row : row + pieces[i].shape[0], columns] = pieces[i][...]


def place_halves(member, pieces):
    spots = [(block, row) for block, row, _ in pieces]
    arrays = [array for _, _, array in pieces]
    rows, half = arrays[0].shape
    return pl.pallas_call(
        functools.partial(place_kernel, spots),
        in_specs=[pl.BlockSpec(memory_space=pltpu.SMEM)]
        + [pl.BlockSpec(memory_space=pltpu.VMEM)] * len(arrays),
        out_specs=pl.BlockSpec(memory_space=pltpu.VMEM),
        out_shape=jax.ShapeDtypeStruct((4, rows, 2 * half), arrays[0].dtype),
        compiler_params=pltpu.CompilerParams(vmem_limit_bytes=VMEM_BYTES),
        cost_estimate=cost(1000),
        name="place_halves",
    )(member.reshape(1), *arrays)


def attn_weight_kernel(
    member_ref, x_ref, all_ref, mixed_ref, q_ref, k_ref, v_ref, branch_ref, out_ref
):
    owner = member_ref[0] ^ pl.program_id(0)
    half = out_ref.shape[2]
    columns = pl.ds(pl.multiple_of((owner % 2) * half, 128), half)
    sources = ((x_ref, q_ref), (all_ref, k_ref), (all_ref, v_ref), (mixed_ref, branch_ref))
    for kind, (left, right) in enumerate(sources):

        @pl.when(owner // 2 == kind)
        def _(left=left, right=right):
            out_ref[0] = dot_tn(left[...], right[:, columns]).astype(BF)


def attn_weight_back(member, *arrays):
    width = arrays[0].shape[1]
    return pl.pallas_call(
        attn_weight_kernel,
        grid=(8,),
        in_specs=[pl.BlockSpec(memory_space=pltpu.SMEM)]
        + [pl.BlockSpec(a.shape, lambda i: (0, 0)) for a in arrays],
        out_specs=pl.BlockSpec((1, width, width // 2), lambda i: (i, 0, 0)),
        out_shape=jax.ShapeDtypeStruct((8, width, width // 2), BF),
        compiler_params=params(),
        cost_estimate=cost(4 * (arrays[0].shape[0] + arrays[1].shape[0]) * width * width),
        name="attn_weight_back",
    )(member.reshape(1), *arrays)


def head_kernel(rows_ref, place_ref, heads_ref, exps_ref, stats_ref, picked_ref):
    rows, place = rows_ref[...], place_ref[...]
    count, words, _ = heads_ref.shape
    picked = 0.0
    for k in range(count):
        scores = dot_nt(heads_ref[k], rows)
        top = jnp.max(scores, axis=0, keepdims=True)
        weights = jnp.exp(scores - top)
        iota = lax.broadcasted_iota(jnp.int32, scores.shape, 0)
        chosen = jnp.where(iota == place - k * words, scores, 0.0)
        picked = picked + jnp.sum(chosen, axis=0, keepdims=True)
        stats_ref[k : k + 1, :] = top
        stats_ref[count + k : count + k + 1, :] = jnp.sum(weights, axis=0, keepdims=True)
        exps_ref[k] = weights.astype(BF)
    picked_ref[...] = picked


def head_forward(rows, place, heads):
    group, width = rows.shape
    count, depth, _ = heads.shape
    block = min(512, group)
    return pl.pallas_call(
        head_kernel,
        grid=(group // block,),
        in_specs=[
            pl.BlockSpec((block, width), lambda i: (i, 0)),
            pl.BlockSpec((1, block), lambda i: (0, i)),
            pl.BlockSpec((count, depth, width), lambda i: (0, 0, 0)),
        ],
        out_specs=[
            pl.BlockSpec((count, depth, block), lambda i: (0, 0, i)),
            pl.BlockSpec((2 * count, block), lambda i: (0, i)),
            pl.BlockSpec((1, block), lambda i: (0, i)),
        ],
        out_shape=[
            jax.ShapeDtypeStruct((count, depth, group), BF),
            jax.ShapeDtypeStruct((2 * count, group), F32),
            jax.ShapeDtypeStruct((1, group), F32),
        ],
        compiler_params=params(),
        cost_estimate=cost(2 * group * width * depth * count),
        name="head_forward",
    )(rows, place, heads)


def chosen_tokens(rank_ref, word_ref, k, turn_no, capacity):
    group = rank_ref.shape[1]
    place = lax.broadcasted_iota(jnp.int32, (capacity, group), 0) + turn_no * capacity
    chosen = rank_ref[k : k + 1, :] == place.astype(F32)
    word = jnp.sum(jnp.where(chosen, word_ref[...] + 1.0, 0.0), axis=1, keepdims=True) - 1.0
    return chosen, word


def word_hots(word, words):
    lanes = lax.broadcasted_iota(jnp.int32, (word.shape[0], words), 1).astype(F32)
    return (word == lanes).astype(BF)


def stats_kernel(sums_ref, out_ref):
    count = sums_ref.shape[0] // 2
    tops = sums_ref[:count, :]
    top = jnp.max(tops, axis=0, keepdims=True)
    out_ref[0:1, :] = top
    out_ref[1:2, :] = jnp.sum(sums_ref[count:, :] * jnp.exp(tops - top), axis=0, keepdims=True)


def scale_kernel(orders, sums_ref, weight_ref, *refs):
    count = sums_ref.shape[0] // 2
    stats, (logsum_ref, scales_ref, columns_ref) = refs[: len(orders)], refs[-3:]
    length = sums_ref.shape[1] // len(orders)
    tops, sums = [], []
    for ref, order in zip(stats, orders):
        pieces = [ref[:, j * length : (j + 1) * length] for j in order]
        together = jnp.concatenate(pieces, axis=1)
        tops.append(together[0:1, :])
        sums.append(together[1:2, :])
    top = functools.reduce(jnp.maximum, tops)
    total = sum(s * jnp.exp(t - top) for s, t in zip(sums, tops))
    logsum = top + jnp.log(total)
    logsum_ref[...] = logsum
    weight = weight_ref[...]
    scales = weight * jnp.exp(sums_ref[:count, :] - logsum)
    scales_ref[...] = jnp.concatenate([scales, weight], axis=0)
    rest = columns_ref.shape[1] - count
    if rest:
        scales = jnp.concatenate([scales, jnp.zeros((rest, weight.shape[1]), F32)], axis=0)
    columns_ref[...] = jnp.transpose(scales)


def head_weight_kernel(exps_ref, rows_ref, columns_ref, terms_ref, out_ref):
    lanes = lax.broadcasted_iota(jnp.int32, columns_ref.shape, 1)
    mine = jnp.where(lanes == pl.program_id(0), columns_ref[...], 0.0)
    scaled = (rows_ref[...].astype(F32) * jnp.sum(mine, axis=1, keepdims=True)).astype(BF)
    out_ref[0] = (dot_nn(exps_ref[0], scaled) - terms_ref[0].astype(F32)).astype(BF)


def head_weight_back(exps, rows, columns, terms):
    count, depth, group = exps.shape
    width = rows.shape[1]
    return pl.pallas_call(
        head_weight_kernel,
        grid=(count,),
        in_specs=[
            pl.BlockSpec((1, depth, group), lambda i: (i, 0, 0)),
            pl.BlockSpec((group, width), lambda i: (0, 0)),
            pl.BlockSpec(columns.shape, lambda i: (0, 0)),
            pl.BlockSpec((1, depth, width), lambda i: (i, 0, 0)),
        ],
        out_specs=pl.BlockSpec((1, depth, width), lambda i: (i, 0, 0)),
        out_shape=jax.ShapeDtypeStruct((count, depth, width), BF),
        compiler_params=params(),
        cost_estimate=cost(2 * group * width * depth * count),
        name="head_weight_back",
    )(exps, rows, columns, terms)


def target_kernel(capacity, rounds_ref, rank_ref, word_ref, weight_ref, rows_ref, out_ref):
    count, words, _ = out_ref.shape

    def term(k, turn_no):
        chosen, word = chosen_tokens(rank_ref, word_ref, k, turn_no, capacity)
        weight = jnp.sum(jnp.where(chosen, weight_ref[...], 0.0), axis=1, keepdims=True)
        found = dot_nn(jnp.where(chosen, 1.0, 0.0).astype(BF), rows_ref[...]) * weight
        return dot_tn(word_hots(word, words), found.astype(BF))

    for k in range(count):
        out_ref[k] = term(k, 0).astype(BF)

    @pl.loop(1, rounds_ref[0])
    def _(turn_no):
        for k in range(count):
            out_ref[k] = (out_ref[k].astype(F32) + term(k, turn_no)).astype(BF)


def whole_call(kernel, out_shape, name, *arrays):
    vmem = pl.BlockSpec(memory_space=pltpu.VMEM)
    smem = pl.BlockSpec(memory_space=pltpu.SMEM)
    return pl.pallas_call(
        kernel,
        in_specs=[smem if a.dtype == jnp.int32 else vmem for a in arrays],
        out_specs=jax.tree.map(lambda _: vmem, out_shape),
        out_shape=out_shape,
        compiler_params=pltpu.CompilerParams(vmem_limit_bytes=VMEM_BYTES),
        cost_estimate=cost(1000),
        name=name,
    )(*arrays)


def head_rows_kernel(scales_ref, place_ref, heads_ref, exps_ref, out_ref):
    count, words, _ = heads_ref.shape
    place, weight = place_ref[...], scales_ref[count : count + 1, :]
    out = None
    for k in range(count):
        grads = exps_ref[k].astype(F32) * scales_ref[k : k + 1, :]
        rows = lax.broadcasted_iota(jnp.int32, grads.shape, 0)
        grads = (grads - jnp.where(rows == place - k * words, weight, 0.0)).astype(BF)
        term = dot_tn(grads, heads_ref[k])
        out = term if out is None else out + term
    out_ref[...] = out.astype(BF)


def head_rows_back(scales, place, heads, exps):
    count, depth, width = heads.shape
    group = exps.shape[2]
    block = min(256, group)
    return pl.pallas_call(
        head_rows_kernel,
        grid=(group // block,),
        in_specs=[
            pl.BlockSpec((count + 1, block), lambda i: (0, i)),
            pl.BlockSpec((1, block), lambda i: (0, i)),
            pl.BlockSpec((count, depth, width), lambda i: (0, 0, 0)),
            pl.BlockSpec((count, depth, block), lambda i: (0, 0, i)),
        ],
        out_specs=pl.BlockSpec((block, width), lambda i: (i, 0)),
        out_shape=jax.ShapeDtypeStruct((group, width), BF),
        compiler_params=params(),
        cost_estimate=cost(2 * group * width * depth * count),
        name="head_rows_back",
    )(scales, place, heads, exps)


def ranks(hits):
    count, length = hits.shape
    cut = hits.reshape(count, length // 128, 128)
    ones = cut.astype(BF)
    before = (jnp.arange(128)[:, None] < jnp.arange(128)[None, :]).astype(BF)
    inner = lax.dot_general(ones, before, (((2,), (0,)), ((), ())), preferred_element_type=F32)
    sums = jnp.sum(ones.astype(F32), axis=2)
    earlier = jnp.arange(length // 128)[:, None] > jnp.arange(length // 128)[None, :]
    outer = jnp.sum(jnp.where(earlier[None], sums[:, None, :], 0.0), axis=2)
    return jnp.where(cut, inner + outer[..., None], -1.0).reshape(count, length)


def split_high_low(values):
    high = lax.reduce_precision(values, 8, 7)
    return high.astype(BF), (values - high).astype(BF)


def body(
    ids,
    targets,
    loss_mask,
    domain_ids,
    expert_lists,
    tables,
    tables_m,
    tables_v,
    attn,
    attn_m,
    attn_v,
    experts,
    experts_m,
    experts_v,
    router,
    router_m,
    router_v,
    gains,
    gains_m,
    gains_v,
):
    shards = lax.axis_size("expert")
    rows_dp = lax.axis_size("dp")
    member = lax.axis_index("expert")
    batch_row = lax.axis_index("dp")
    group = ids.shape[0]
    local = group // shards
    own = member * local
    width = gains.shape[1]
    slots = expert_lists.shape[3]
    words = tables.shape[1]
    order = block_order()

    attn_b = attn.astype(BF)
    if quick_expert() and quick_dp():
        mine = lax.dynamic_slice(
            attn_b,
            (member // 2, 0, (member % 2) * (width // 2)),
            (1, attn.shape[1], width // 2),
        )[0]
        below, above = turn(mine, 1), turn(mine, -1)
        attn_parts = jnp.stack([mine, below, turn(below, 1), above])
        attn_parts = attn_parts[slot_shards()].reshape(width, width // 2)
        attn_pieces = gather_pieces(attn_parts)
    table_b = tables[0].astype(BF)
    experts_b = experts[0].astype(BF)
    head_b = tables[1].astype(BF)

    capacity = min(group, 3 * group // (2 * shards * rows_dp))
    capacity = -(-capacity // 16) * 16
    ids_dp = jnp.stack([ids] + [turn(ids, k) for k in range(1, rows_dp)])
    first_word = (member * rows_dp + batch_row) * words
    ids_own = ids_dp - first_word
    rank_own = ranks((ids_own >= 0) & (ids_own < words))
    ids_own = ids_own.astype(F32)
    place = jnp.arange(capacity, dtype=F32)
    owners = (batch_row + jnp.arange(rows_dp)) % rows_dp
    ids_from = ids[None, :] - ((member * rows_dp + owners) * words)[:, None]
    rank_from = ranks((ids_from >= 0) & (ids_from < words))
    rank_from = rank_from.reshape(rows_dp, shards, local)[:, order].reshape(rows_dp, group)
    owner_of = ids_dp // words
    owner_hits = owner_of[:, None, :] == jnp.arange(shards * rows_dp)[None, :, None]
    most = jnp.max(jnp.sum(owner_hits.astype(F32), axis=2)).astype(jnp.int32)
    rounds = (most + capacity - 1) // capacity

    def own_select(turn_no):
        chosen = rank_own[:, None, :] == (place + turn_no * capacity)[None, :, None]
        at = jnp.sum(jnp.where(chosen, ids_own[:, None, :] + 1.0, 0.0), axis=2) - 1.0
        at = at.reshape(-1)[:, None]
        return (at == jnp.arange(words, dtype=F32)[None, :]).astype(BF)

    def from_select(turn_no):
        chosen = rank_from[:, None, :] == (place + turn_no * capacity)[None, :, None]
        return chosen.reshape(-1, group).astype(BF)

    def look_up(select_own):
        found = dot_nn(select_own, table_b).astype(BF).reshape(rows_dp, capacity, width)
        arrived = [found[0]] + [turn(found[k], -k) for k in range(1, rows_dp)]
        return jnp.concatenate(arrived)

    def put(arrived, select_from):
        return dot_tn(select_from, arrived).astype(BF)

    def spread(turn_no, grads, select_own, select_from, earlier=None):
        chosen = dot_nn(select_from, grads).astype(BF).reshape(rows_dp, capacity, width)
        arrived = [chosen[0]] + [turn(chosen[k], k) for k in range(1, rows_dp)]
        return dot_tn(select_own, jnp.concatenate(after(arrived, earlier)))

    targets_mine = targets.reshape(shards, local)[order].reshape(-1)
    word = targets_mine - member * (rows_dp * words)
    word_slot = jnp.where((word >= 0) & (word < rows_dp * words), word // words, rows_dp)
    word_row = (word % words).astype(F32)[None, :]
    word_hits = word_slot[None, :] == jnp.arange(rows_dp)[:, None]
    word_rank = ranks(word_hits)
    word_most = jnp.max(jnp.sum(word_hits.astype(F32), axis=1)).astype(jnp.int32)
    word_rounds = ((word_most + capacity - 1) // capacity).reshape(1)

    def token_weights():
        everything = loss_mask.shape[0]
        domain_of = jnp.take(domain_ids, jnp.arange(everything) // SEQ)
        hits = ((domain_of[:, None] == jnp.arange(NDOM)[None, :]) & (loss_mask[:, None] > 0)).astype(
            F32
        )
        counts = jnp.sum(hits, axis=0)
        domain_weight = 10.0 * (NDOM - jnp.arange(NDOM)).astype(F32) / jnp.maximum(counts, 1.0)
        group_hits = lax.dynamic_slice_in_dim(hits, batch_row * group, group, 0)
        group_hits = group_hits.reshape(shards, local, NDOM)[order].reshape(group, NDOM)
        token_weight = jnp.sum(group_hits * domain_weight[None, :], axis=1)
        return token_weight, group_hits, counts

    token_weight, group_hits, counts = token_weights()
    lists = expert_lists[0, 0][order]
    hot = lists[:, :, None] == jnp.arange(local)[None, None, :]
    hot_b = hot.reshape(-1, local).astype(BF)
    select_own = own_select(0)
    select_from = from_select(0)
    quick = quick_expert() and quick_dp()
    arrived = look_up(select_own)
    expert_shards = lax.all_gather(experts_b, "dp")
    looked = put(arrived, select_from)
    _, looked = lax.while_loop(
        lambda state: state[0] < rounds,
        lambda state: (
            state[0] + 1,
            state[1]
            + put(
                look_up(own_select(state[0].astype(F32))),
                from_select(state[0].astype(F32)),
            ),
        ),
        (jnp.int32(1), looked),
    )
    if quick_expert() and quick_dp():
        attn_full = place_halves(member, attn_pieces)
    else:
        attn_full = lax.all_gather(attn_b, "dp", axis=1, tiled=True)
    embedded = sum_blocks(split_blocks(looked))
    router_b = router.astype(BF)

    normed_ab = normed(embedded, gains[0]).astype(BF)
    normed_all = gather_rows(normed_ab)
    queries = dot_nn(normed_ab, attn_full[0]).astype(BF)
    keys = dot_nn(normed_all, attn_full[1]).astype(BF)
    values = dot_nn(normed_all, attn_full[2]).astype(BF)
    token_place = (order[:, None] * local + jnp.arange(local)[None, :]).reshape(-1)
    seq_start = own // SEQ * SEQ
    key_place = jnp.where(token_place >= seq_start, token_place, group)[:, None]
    query_place = (own + jnp.arange(local))[None, :]
    mixed_b, logsum = attend(queries, keys, values, key_place, query_place)
    resid_one = embedded + dot_nn(mixed_b, attn_full[3])

    normed_bb = normed(resid_one, gains[1]).astype(BF)
    router_logits = dot_nn(normed_bb, router_b)
    gates = jax.nn.softmax(router_logits, axis=-1)
    gates_mine = jnp.transpose(gates[:, order])
    gate_table = jnp.where(hot, gates_mine[:, None, :], 0.0)
    slot_gates = jnp.sum(gate_table, axis=2).reshape(-1, 1)
    gate_high, gate_low = split_high_low(gate_table.reshape(-1, local))
    send = dot_nn(hot_b, normed_bb).astype(BF)
    received = exchange(split_blocks(send))
    head_shards = lax.all_gather(after(head_b, (expert_shards, received[1])), "dp")
    received = jnp.concatenate(received)
    pres, hiddens, produced = [], [], None
    for shard in expert_shards:
        pre = dot_nn(received, shard[0])
        hidden = gelu(pre).astype(BF)
        term = dot_nt(hidden, shard[1])
        produced = term if produced is None else produced + term
        pres.append(pre)
        hiddens.append(hidden)
    returned = jnp.concatenate(exchange(split_blocks(produced.astype(BF))))
    mixture = dot_tn(gate_high, returned) + dot_tn(gate_low, returned)
    resid_two = resid_one + mixture
    normed_cb = normed(resid_two, gains[2]).astype(BF)

    rows_all = gather_rows(normed_cb)
    target_terms = whole_call(
        functools.partial(target_kernel, capacity),
        jax.ShapeDtypeStruct((rows_dp, words, width), BF),
        "target_terms",
        word_rounds,
        word_rank,
        word_row,
        token_weight[None, :],
        rows_all,
    )
    word_place = jnp.where(word_slot < rows_dp, word_slot * words + word % words, -1)[None, :]
    exps, head_stats, picked = head_forward(
        after(rows_all, target_terms), word_place, head_shards
    )
    stats = whole_call(
        stats_kernel, jax.ShapeDtypeStruct((2, group), F32), "head_stats", head_stats
    )
    if quick_expert():
        gathered = [stats] + [swap(stats, k, "expert") for k in range(1, 8)]
        orders = [[j ^ k for j in range(8)] for k in range(8)]
    else:
        gathered = list(lax.all_gather(stats, "expert"))
        orders = [list(range(shards))] * shards
    logsum_tok, scales, columns = whole_call(
        functools.partial(scale_kernel, orders),
        (
            jax.ShapeDtypeStruct((1, group), F32),
            jax.ShapeDtypeStruct((rows_dp + 1, group), F32),
            jax.ShapeDtypeStruct((group, -(-rows_dp // 8) * 8), F32),
        ),
        "head_scales",
        head_stats,
        token_weight[None, :],
        *gathered,
    )
    own_block = 0 if quick_expert() else member
    grad_rows_c = head_rows_back(scales, word_place, head_shards, exps)
    grad_heads = head_weight_back(exps, rows_all, columns, target_terms)
    grad_head = sum_shards(grad_heads)
    own_sums = jnp.sum(
        lax.dynamic_slice_in_dim(group_hits, own_block * local, local, 0)
        * lax.dynamic_slice_in_dim(logsum_tok[0], own_block * local, local, 0)[:, None],
        axis=0,
    ) - jnp.sum(group_hits * picked[0][:, None], axis=0)
    grad_normed_c = sum_blocks(split_blocks(grad_rows_c))
    grad_two, grad_gain_c = norm_back(resid_two, gains[2], grad_normed_c)

    two_high, two_low = split_high_low(grad_two)
    grad_slot = dot_nn(hot_b, two_high) + dot_nn(hot_b, two_low)
    grad_gate_slot = jnp.sum(grad_slot * returned.astype(F32), axis=-1)
    grad_produced = jnp.concatenate(
        exchange(split_blocks((grad_slot * slot_gates).astype(BF)))
    )
    grad_pres, grad_sent = [], None
    for k in range(rows_dp):
        grad_hidden = dot_nn(grad_produced, expert_shards[k, 1])
        _, gelu_pull = jax.vjp(gelu, pres[k])
        grad_pres.append(gelu_pull(grad_hidden)[0].astype(BF))
        term = dot_nt(grad_pres[k], expert_shards[k, 0])
        grad_sent = term if grad_sent is None else grad_sent + term
    grad_sent = grad_sent.astype(BF)
    late_produced, late_received = after((grad_produced, received), grad_sent)
    grad_parts = []
    for grad_pre, hidden in zip(grad_pres, hiddens):
        grad_parts.append(dot_tn(late_received, grad_pre).astype(BF))
        grad_parts.append(dot_tn(late_produced, hidden).astype(BF))
    grad_parts = jnp.stack(grad_parts).reshape(rows_dp, 2, width, -1)
    grad_experts = sum_shards(grad_parts)[None]
    grad_back = jnp.concatenate(exchange(split_blocks(grad_sent)))
    grad_normed_b = dot_tn(hot_b, grad_back)
    grad_gates = jnp.sum(
        jnp.where(hot, grad_gate_slot.reshape(shards, slots)[:, :, None], 0.0), axis=1
    )
    grad_gates = jnp.transpose(grad_gates[order])
    _, soft_pull = jax.vjp(lambda logit_rows: jax.nn.softmax(logit_rows, axis=-1), router_logits)
    grad_router_logits = soft_pull(grad_gates)[0].astype(BF)
    grad_router = dot_tn(normed_bb, grad_router_logits)
    grad_normed_b = grad_normed_b + dot_nt(grad_router_logits, router_b)
    normal_back, grad_gain_b = norm_back(resid_one, gains[1], grad_normed_b)
    grad_one = grad_two + normal_back

    grad_branch = grad_one.astype(BF)
    grad_mixed = dot_nt(grad_branch, attn_full[3]).astype(BF)
    grad_query, grad_keys, grad_values = attend_back(
        queries, keys, values, grad_mixed, mixed_b, logsum, key_place, query_place
    )
    grad_normed_rows = dot_nt(grad_keys, attn_full[1]) + dot_nt(grad_values, attn_full[2])
    firsts = []
    grad_normed_a = sum_blocks(split_blocks(grad_normed_rows.astype(BF)), firsts)
    grad_normed_a = grad_normed_a + dot_nt(grad_query, attn_full[0])
    normal_front, grad_gain_a = norm_back(embedded, gains[0], grad_normed_a)
    grad_embedded = (grad_one + normal_front).astype(BF)
    grad_embedded_all = gather_rows(grad_embedded)
    if quick_expert() and quick_dp():
        blocks = attn_weight_back(
            member,
            normed_ab,
            after(normed_all, firsts[0]),
            mixed_b,
            grad_query,
            grad_keys,
            grad_values,
            grad_branch,
        )
        blocks = after(blocks, grad_embedded_all)
        part = sum_blocks([blocks[j] for j in range(8)]).astype(BF)
        part = part.reshape(4, width // 4, width // 2)[slot_shards()]
        part = sum_turns([part[k] for k in range(4)])
        attn_ready = part
        attn_squares = jnp.sum(part * part)
        grad_attn = place_halves(member, gather_pieces(part.astype(BF)))
    else:
        attn_ready = None
        grad_attn = jnp.stack(
            [
                dot_tn(normed_ab, grad_query),
                dot_tn(normed_all, grad_keys),
                dot_tn(normed_all, grad_values),
                dot_tn(mixed_b, grad_branch),
            ]
        ).astype(BF)
        grad_attn = lax.psum_scatter(grad_attn, "dp", scatter_dimension=1, tiled=True)
        grad_attn = lax.psum(grad_attn, "expert")
        attn_squares = jnp.sum(jnp.square(grad_attn.astype(F32))) / shards
    grad_embed = spread(0, grad_embedded_all, select_own, select_from, attn_ready)
    _, grad_embed = lax.while_loop(
        lambda state: state[0] < rounds,
        lambda state: (
            state[0] + 1,
            state[1]
            + spread(
                state[0],
                grad_embedded_all,
                own_select(state[0].astype(F32)),
                from_select(state[0].astype(F32)),
            ),
        ),
        (jnp.int32(1), grad_embed),
    )
    small = jnp.concatenate(
        [grad_router.reshape(-1), grad_gain_a, grad_gain_b, grad_gain_c, own_sums]
    )
    head_squares = jnp.sum(jnp.square(grad_head.astype(F32)))
    small = jnp.pad(small, (0, -small.shape[0] % 1024)).reshape(-1, 128)
    small = sum_everywhere(small).reshape(-1)
    edge = router.size
    grad_router = small[:edge].reshape(router.shape)
    grad_gains = small[edge : edge + 3 * width].reshape(3, width)
    domain_sums = small[edge + 3 * width : edge + 3 * width + NDOM]
    small_squares = jnp.sum(grad_router * grad_router) + jnp.sum(grad_gains * grad_gains)
    grad_experts = after(grad_experts, head_squares)
    grad_experts = grad_experts.astype(F32)
    squares = (
        jnp.sum(grad_embed * grad_embed)
        + head_squares
        + jnp.sum(grad_experts * grad_experts)
        + attn_squares
    )
    squares = sum_everywhere(jnp.broadcast_to(squares, (1, 128)))[0, 0]
    grad_norm = jnp.sqrt(squares + small_squares)
    factor = jnp.minimum(1.0, CLIP / (grad_norm + 1e-06))
    grad_tables = jnp.stack([grad_embed, grad_head.astype(F32)])
    tables_out = adam(tables, grad_tables * factor, tables_m, tables_v, 0.1, 0.01)
    attn_out = adam(attn, grad_attn.astype(F32) * factor, attn_m, attn_v, 0.1, 0.01)
    experts_out = adam(experts, grad_experts * factor, experts_m, experts_v, 0.1, 0.01)
    router_out = adam(router, grad_router * factor, router_m, router_v, 0.04, 0.01)
    gains_out = adam(gains, grad_gains * factor, gains_m, gains_v, 0.4, 0.0)
    return (
        domain_sums,
        counts,
        grad_norm,
        *tables_out,
        *attn_out,
        *experts_out,
        *router_out,
        *gains_out,
    )


def solution(mesh):
    table = P(None, ("expert", "dp"), None)
    attn = P(None, "dp", None)
    expert = P("expert", None, None, "dp")
    in_specs = (
        P("dp"),
        P("dp"),
        P(),
        P(),
        P("dp", "expert", None, None),
        *[table] * 3,
        *[attn] * 3,
        *[expert] * 3,
        *[P()] * 6,
    )
    out_specs = (*[P()] * 3, *[table] * 4, *[attn] * 4, *[expert] * 4, *[P()] * 8)
    return jax.shard_map(body, mesh=mesh, in_specs=in_specs, out_specs=out_specs, check_vma=False)
```
